32 devices in a mesh: seq: 16 (over z, y, x), chan: 2 (over core).
Axes of the slice: x: 2, y: 2, z: 4, core: 2. Of those that a mesh axis runs over, the one named last changes fastest.
Arguments:
- streams: bfloat16 [3, 4096, 8192], P(None, 'seq', 'chan'), may hold values from -6 to 6
- short_filter: float32 [3, 3, 8192], P(None, None, 'chan'), may hold values from -3 to 3
- pole_rates: float32 [16, 8192], P(None, 'chan'), may hold values from 2.4414063e-05 to 0.03
- residues: float32 [16, 8192], P(None, 'chan'), may hold values from -3 to 3
- direct: float32 [8192], P('chan'), may hold values from -3 to 3
- doc_lengths: int32 [4], replicated, may hold values from 1 to 2048, 4096 in all
- targets: int32 [4096], P('seq'), may hold values from 0 to 511
- unembed: bfloat16 [8192, 512], P('chan'), may hold values from -0.7 to 0.7
Outputs:
- gated_out: bfloat16 [4096, 8192], P('seq', 'chan')
- token_loss: float32 [4096], P('seq')
The draws below stay inside these ranges and needn't reach their ends.
All inputs are finite; a program needn't handle non-finite values.
Results may differ from the reference program's by a relative error of at most 0.012.
Values may be sent and summed in bfloat16 or wider, within the bound.
A program may use at most 128 MiB of HBM per device.

```python
import math
import jax
import jax.numpy as jnp
import numpy as np
from jax import lax

D = 8192
POLES = 16
VOCAB = 512
TAPS = 3
DOCS = 4
TOKENS = 4096


def draw_unembed(key, part):
    key = jax.random.fold_in(key, 7)
    key_vals = jax.random.fold_in(key, 0)
    col_scale = 8.0
    base_vals = jnp.clip(jax.random.normal(key_vals, (D, VOCAB), jnp.float32), -4.0, 4.0)
    scaled = jnp.clip(base_vals * col_scale * (1.5 / math.sqrt(D)), -0.7, 0.7)
    return scaled.astype(jnp.bfloat16)


def with_ends(drawn, rng, least, high):
    extent = drawn.shape
    spot = [jax.random.randint(jax.random.fold_in(rng, axis), (), 0, extent[axis]) for axis in range(len(extent))]
    drawn = drawn.at[tuple(spot)].set(least)
    longest = extent.index(max(extent))
    spot[longest] = (spot[longest] + 1) % extent[longest]
    return drawn.at[tuple(spot)].set(high)


def block_scale(key, shape, pieces, low, high):
    gain = 1.0
    for dim, parts in pieces:
        steps = jax.random.uniform(jax.random.fold_in(jax.random.fold_in(key, 6), dim), (parts,), jnp.float32, low / len(pieces), high / len(pieces))
        gain = gain * jnp.repeat(jnp.exp(steps), shape[dim] // parts).reshape((-1,) + (1,) * (len(shape) - 1 - dim))
    return gain


def cumulative_ranks(number_of, lean):
    weights = [(1 << 20) // math.isqrt(standing ** lean) + 1 for standing in range(1, number_of + 1)]
    spread = 1 + sum(weights) // (1 << 30)
    return np.cumsum(np.array([max(1, weight // spread) for weight in weights]))


def skewed_ids(stream_key, shape, count, lean):
    grid = cumulative_ranks(count, lean)
    ticket = jax.random.randint(jax.random.fold_in(stream_key, 1), shape, 0, int(grid[count - 1]))
    grade = jnp.searchsorted(jnp.asarray(grid, jnp.int32), ticket, side="right")
    return jax.random.permutation(jax.random.fold_in(stream_key, 2), count)[grade].astype(jnp.int32)


def split_up(amount, total, reach, skew):
    portions = [(1 << 20) // math.isqrt(grade ** skew) + 1 for grade in range(2, amount + 1)]
    surplus, given = total - reach - (amount - 1), [1] * (amount - 1)
    while surplus > 0:
        candidates = [i for i in range(amount - 1) if given[i] < reach]
        pool, left = sum([portions[i] for i in candidates]), surplus
        for i in candidates:
            more = min(reach - given[i], max(1, left * portions[i] // pool), surplus)
            given[i] = given[i] + more
            surplus = surplus - more
    return np.array([reach] + given)


def uneven(key, number_of, total, most, slope):
    if number_of == 2:
        one = jax.random.randint(key, (), max(1, total - most), min(most, total - 1) + 1)
        return jnp.stack([one, total - one])
    sizes = jnp.asarray(split_up(number_of, total, most, slope), jnp.int32)
    twos = (number_of - 1) // 2
    giver, taker = sizes[1:1 + 2 * twos:2], sizes[2:2 + 2 * twos:2]
    slack = jnp.minimum(giver - 1, most - taker)
    passed = jax.random.randint(jax.random.fold_in(key, 1), (twos,), 0, 1 << 20) % (slack + 1)
    sizes = sizes.at[1:1 + 2 * twos:2].set(giver - passed).at[2:2 + 2 * twos:2].set(taker + passed)
    return sizes[jax.random.permutation(jax.random.fold_in(key, 2), number_of)]


def bell_draw(own_key, extent, scale, bound, cuts=(), held_as=jnp.bfloat16):
    factor_of = block_scale(own_key, extent, cuts, -0.22, 0.18) if cuts else 1.0
    values = jax.random.normal(own_key, extent, jnp.float32) * scale * factor_of
    return jnp.minimum(jnp.maximum(values, -bound), bound).astype(held_as)


def setup_inputs(seed: int = 0) -> dict:
    keys = jax.random.split(jax.random.key(seed), 9)
    streams = bell_draw(keys[0], (3, TOKENS, D), 1.0, 6.0, ((1, 16), (2, 2)))
    short_filter = bell_draw(keys[1], (3, TAPS, D), 0.6, 3.0, ((2, 2),), jnp.float32)
    pole_rates = jnp.clip(jnp.exp(math.log(0.03) - 7.1137933 * jax.random.uniform(keys[2], (POLES, D), jnp.float32) ** block_scale(keys[2], (POLES, D), ((1, 2),), -0.2, 0.2)), 2.441406286379788e-05, 0.03)
    residues = bell_draw(keys[3], (POLES, D), 0.5, 3.0, ((1, 2),), jnp.float32)
    direct = bell_draw(keys[4], (D,), 0.5, 3.0, ((0, 2),), jnp.float32)
    doc_lengths = uneven(keys[5], DOCS, TOKENS, TOKENS // 2, 0).astype(jnp.int32)
    targets = with_ends(skewed_ids(keys[6], (TOKENS,), VOCAB, 2), jax.random.fold_in(keys[6], 3), 0, VOCAB - 1).astype(jnp.int32)
    unembed = draw_unembed(jax.random.fold_in(keys[8], 71), 0)
    return {"streams": streams, "short_filter": short_filter, "pole_rates": pole_rates, "residues": residues, "direct": direct, "doc_lengths": doc_lengths, "targets": targets, "unembed": unembed}


def starts_of(doc_lengths, position):
    doc_first = jnp.cumsum(doc_lengths) - doc_lengths
    chosen = jnp.where(doc_first[None, :] <= position[:, None], doc_first[None, :], 0)
    return jnp.max(chosen, axis=1).astype(jnp.int32)


def reference(streams, short_filter, pole_rates, residues, direct, doc_lengths, targets, unembed):
    position = jnp.arange(TOKENS, dtype=jnp.int32)
    doc_start = starts_of(doc_lengths, position)
    widened = streams.astype(jnp.float32)
    filtered = short_filter[:, 0, None, :] * widened
    for shift_by in range(1, TAPS):
        moved = jnp.pad(widened, ((0, 0), (shift_by, 0), (0, 0)))[:, :TOKENS]
        in_doc = (position - shift_by >= doc_start).astype(jnp.float32)
        filtered = filtered + short_filter[:, shift_by, None, :] * moved * in_doc[None, :, None]
    driver = filtered[1] * filtered[2]
    decay = jnp.exp(-pole_rates)
    inflow = 1.0 - decay
    keep_state = (doc_start < position).astype(jnp.float32)

    def advance(state, inputs):
        drive_row, keep_row = inputs
        state = decay * keep_row * state + inflow * drive_row[None, :]
        return state, jnp.sum(residues * state, axis=0)

    _, long_out = lax.scan(advance, jnp.zeros((POLES, D), jnp.float32), (driver, keep_state))
    gated_out = (filtered[0] * (long_out + direct[None, :] * driver)).astype(jnp.bfloat16)
    logits = jnp.dot(gated_out, unembed, preferred_element_type=jnp.float32)
    peak = jnp.max(logits, axis=1)
    exp_total = jnp.sum(jnp.exp(logits - peak[:, None]), axis=1)
    vocab_ids = jnp.arange(VOCAB, dtype=jnp.int32)
    picked = jnp.sum(jnp.where(targets[:, None] == vocab_ids[None, :], logits, 0.0), axis=1)
    return gated_out, peak + jnp.log(exp_total) - picked
```

```python
import functools

import jax
import jax.numpy as jnp
from jax import lax
from jax.experimental import pallas as pl
from jax.experimental.pallas import tpu as pltpu
from jax.sharding import PartitionSpec as P

MESH = pl.DeviceIdType.MESH
LANES = 128
GROUP = 8 * LANES
VMEM_LIMIT = 48 * 1024 * 1024


def doc_firsts(lengths_ref):
    firsts = [jnp.int32(0)]
    for d in range(lengths_ref.shape[0] - 1):
        firsts.append(firsts[-1] + lengths_ref[d])
    return firsts


def any_between(firsts, low, high):
    found = jnp.bool_(False)
    for first in firsts:
        found = found | ((first >= low) & (first < high))
    return found


def greet(peers):
    barrier = pltpu.get_barrier_semaphore()
    for axis, peer, there in peers:

        @pl.when(there)
        def _():
            pl.semaphore_signal(barrier, inc=1, device_id={axis: peer}, device_id_type=MESH)

    if peers:
        pl.semaphore_wait(barrier, sum(jnp.where(there, 1, 0) for _, _, there in peers))


def edge_kernel(blocks, tail_ref, out_ref, packed, landed, send_sem, recv_sem):
    me = lax.axis_index("seq")
    half = packed.shape[1]
    greet((("seq", me + 1, me < blocks - 1), ("seq", me - 1, me > 0)))
    rows = []
    for side in range(2):
        cols = pl.ds(side * half, half)
        for j in range(3):
            rows.append(tail_ref[j, :, cols].astype(jnp.float32)[14:16])
        rows.append(jnp.zeros((2, half), jnp.float32))
    packed[...] = jnp.concatenate(rows, axis=0).astype(jnp.bfloat16)
    copy = pltpu.make_async_remote_copy(
        src_ref=packed,
        dst_ref=landed,
        send_sem=send_sem,
        recv_sem=recv_sem,
        device_id={"seq": me + 1},
        device_id_type=MESH,
    )

    @pl.when(me < blocks - 1)
    def _():
        copy.start()

    @pl.when(me > 0)
    def _():
        copy.wait_recv()
        got = landed[...].astype(jnp.float32)
        out_ref[:, pl.ds(0, half)] = got[0:8]
        out_ref[:, pl.ds(half, half)] = got[8:16]

    @pl.when(me == 0)
    def _():
        out_ref[...] = jnp.zeros_like(out_ref)

    @pl.when(me < blocks - 1)
    def _():
        copy.wait_send()


def load_extended(ext, stream_ref, edge_ref, stream_id):
    block_len = stream_ref.shape[1]
    pitch = block_len + 8
    for ct in range(8):
        edge = edge_ref[:, pl.ds(ct * LANES, LANES)]
        both = jnp.concatenate([edge[0:6], edge[2 * stream_id : 2 * stream_id + 2]], axis=0)
        ext[pl.ds(ct * pitch, 8), :] = both

    def step(i, _):
        rows = pl.ds(pl.multiple_of(i * 16, 16), 16)
        for ct in range(8):
            tile = stream_ref[0, rows, pl.ds(ct * LANES, LANES)].astype(jnp.float32)
            ext[pl.ds(pl.multiple_of(ct * pitch + i * 16 + 8, 8), 16), :] = tile
        return 0

    lax.fori_loop(0, block_len // 16, step, 0)


def taps_of(ext, filter_ref, stream_id, i, ct, masks):
    cols = pl.ds(ct * LANES, LANES)
    pitch = ext.shape[0] // 8
    terms = []
    for shift in range(3):
        tap = filter_ref[stream_id, shift : shift + 1, cols]
        rows = pl.ds(ct * pitch + i * 8 + (8 - shift), 8)
        term = tap * ext[rows, :]
        if shift and masks is not None:
            term = jnp.where(masks[shift - 1], term, 0.0)
        terms.append(term)
    return terms[0] + terms[1] + terms[2]


def tile_masks(firsts, base):
    pos = base + lax.broadcasted_iota(jnp.int32, (8, LANES), 0)
    start = jnp.zeros((8, LANES), jnp.int32)
    for first in firsts:
        start = jnp.maximum(start, jnp.where(first <= pos, first, 0))
    return [pos - shift >= start for shift in (1, 2)]


def to_sublanes(ref, scratch, row_count):
    for top in range(0, row_count, 8):
        for ct in range(8):
            scratch[pl.ds(top * 8 + ct * 8, 8), :] = ref[top : top + 8, pl.ds(ct * LANES, LANES)]
    return [scratch[pl.ds((p // 8) * 64 + p % 8, 8, stride=8), :] for p in range(row_count)]


def local_kernel(
    lengths_ref, k_ref, v_ref, edge_ref, filter_ref, rate_ref, residue_ref, direct_ref,
    y_ref, end_ref, rate_out, weight_out,
    ext_k, ext_v, turn, driver,
):
    block_len = k_ref.shape[1]
    poles = rate_ref.shape[0]
    first_pos = lax.axis_index("seq") * block_len
    firsts = doc_firsts(lengths_ref)
    load_extended(ext_k, k_ref, edge_ref, 1)
    load_extended(ext_v, v_ref, edge_ref, 2)

    def filter_step(i, _):
        base = first_pos + i * 8

        def fill(masks):
            for ct in range(8):
                k = taps_of(ext_k, filter_ref, 1, i, ct, masks)
                v = taps_of(ext_v, filter_ref, 2, i, ct, masks)
                driver[pl.ds(pl.multiple_of(i * 64 + ct * 8, 8), 8), :] = k * v

        near = any_between(firsts, base - 1, base + 8)

        @pl.when(near)
        def _():
            fill(tile_masks(firsts, base))

        @pl.when(jnp.logical_not(near))
        def _():
            fill(None)

        return 0

    lax.fori_loop(0, block_len // 8, filter_step, 0)

    rates = to_sublanes(rate_ref, turn, poles)
    decays = [jnp.exp(-r) for r in rates]
    for p in range(poles):
        rate_out[p, 0] = rates[p]
    residues = to_sublanes(residue_ref, turn, poles)
    weights = [residues[p] * (1.0 - decays[p]) for p in range(poles)]
    for p in range(poles):
        weight_out[p, 0] = weights[p]
    for ct in range(8):
        turn[pl.ds(ct * 8, 8), :] = jnp.broadcast_to(direct_ref[:, pl.ds(ct * LANES, LANES)], (8, LANES))
    direct = turn[pl.ds(0, 8, stride=8), :]

    def chunk(i, states):
        base = first_pos + i * 8

        def run(states, with_reset):
            states = list(states)
            for j in range(8):
                x = driver[pl.ds(i * 64 + j, 8, stride=8), :]
                if with_reset:
                    hit = any_between(firsts, base + j, base + j + 1)
                    keep = jnp.where(hit, 0.0, 1.0)
                sums = [direct * x, None, None, None]
                for p in range(poles):
                    held = states[p] * keep if with_reset else states[p]
                    states[p] = decays[p] * held + x
                    term = weights[p] * states[p]
                    sums[p % 4] = term if sums[p % 4] is None else sums[p % 4] + term
                y_ref[0, pl.ds(i * 64 + j, 8, stride=8), :] = (sums[0] + sums[1]) + (sums[2] + sums[3])
            return tuple(states)

        return lax.cond(
            any_between(firsts, base, base + 8),
            lambda s: run(s, True),
            lambda s: run(s, False),
            states,
        )

    zeros = tuple(jnp.zeros((8, LANES), jnp.float32) for _ in range(poles))
    states = lax.fori_loop(0, block_len // 8, chunk, zeros)
    for p in range(poles):
        end_ref[p, 0] = states[p]


def exchange_kernel(blocks, block_len, pieces, lengths_ref, rate_ref, end_ref, in_ref, outbox, inbox, send_sem, recv_sem):
    me = lax.axis_index("seq")
    first_pos = me * block_len
    rounds = max(1, (blocks - 1).bit_length())
    peers = []
    for k in range(rounds):
        peers.append(("seq", me + (1 << k), me + (1 << k) < blocks))
        peers.append(("seq", me - (1 << k), me >= (1 << k)))
    greet(peers)
    firsts = doc_firsts(lengths_ref)

    def last_start(pos):
        best = jnp.int32(0)
        for first in firsts:
            best = jnp.maximum(best, jnp.where(first <= pos, first, 0))
        return best

    own_keep = jnp.where(last_start(first_pos + block_len - 1) < first_pos, 1.0, 0.0)
    span = end_ref.shape[0] // pieces

    def copy(k, piece):
        rows = pl.ds(piece * span, span)
        return pltpu.make_async_remote_copy(
            src_ref=outbox.at[k, rows],
            dst_ref=inbox.at[k, rows],
            send_sem=send_sem.at[k, piece],
            recv_sem=recv_sem.at[k, piece],
            device_id={"seq": me + (1 << k)},
            device_id_type=MESH,
        )

    in_ref[...] = jnp.zeros_like(in_ref)
    for k in range(rounds):
        reach = 1 << k
        far = first_pos - (reach - 1) * block_len
        for piece in range(pieces):
            rows = pl.ds(piece * span, span)

            @pl.when(me + reach < blocks)
            def _():
                whole = end_ref[rows, :]
                if k:
                    fade = jnp.exp(-rate_ref[rows, :] * float(block_len)) * own_keep
                    whole = whole + fade * in_ref[rows, :]
                outbox[k, rows, :] = whole.astype(jnp.bfloat16)
                copy(k, piece).start()

        if k:
            clear = jnp.where(last_start(first_pos - 1) < far, 1.0, 0.0)
        for piece in range(pieces):
            rows = pl.ds(piece * span, span)

            @pl.when(me >= reach)
            def _():
                copy(k, piece).wait_recv()
                got = inbox[k, rows, :].astype(jnp.float32)
                if k:
                    fade = jnp.exp(-rate_ref[rows, :] * float((reach - 1) * block_len))
                    got = got * (fade * clear)
                in_ref[rows, :] += got

    for k in range(rounds):
        for piece in range(pieces):

            @pl.when(me + (1 << k) < blocks)
            def _():
                copy(k, piece).wait_send()


def finish_kernel(
    lengths_ref, q_ref, edge_ref, filter_ref, rate_ref, weight_ref, in_ref, y_in, unembed_ref,
    gated_ref, logits_ref,
    ext_q, y, total,
):
    block_len = q_ref.shape[1]
    poles = rate_ref.shape[0]
    first_pos = lax.axis_index("seq") * block_len
    firsts = doc_firsts(lengths_ref)
    group = pl.program_id(0)
    cut = jnp.int32(block_len)
    for first in firsts:
        cut = jnp.where(first >= first_pos, jnp.minimum(cut, first - first_pos), cut)
    load_extended(ext_q, q_ref, edge_ref, 0)
    decays = [jnp.exp(-rate_ref[p, 0]) for p in range(poles)]
    fading = tuple(weight_ref[p, 0] * in_ref[p, 0] * decays[p] for p in range(poles))

    def fade_chunk(i, fading):
        fading = list(fading)
        for j in range(8):
            sums = [fading[0], fading[1], fading[2], fading[3]]
            for p in range(4, poles):
                sums[p % 4] = sums[p % 4] + fading[p]
            arrived = (sums[0] + sums[1]) + (sums[2] + sums[3])
            rows = pl.ds(i * 64 + j, 8, stride=8)
            y[rows, :] = y_in[0, rows, :] + jnp.where(i * 8 + j < cut, 1.0, 0.0) * arrived
            fading = [f * d for f, d in zip(fading, decays)]
        return tuple(fading)

    carried = (cut + 7) // 8
    lax.fori_loop(0, carried, fade_chunk, fading)

    def plain_chunk(i, _):
        rows = pl.ds(pl.multiple_of(i * 64, 64), 64)
        y[rows, :] = y_in[0, rows, :]
        return 0

    lax.fori_loop(carried, block_len // 8, plain_chunk, 0)

    def gate_step(i, _):
        base = first_pos + i * 16

        def fill(masked):
            for ct in range(8):
                halves = []
                for side in range(2):
                    tile = i * 2 + side
                    masks = tile_masks(firsts, base + side * 8) if masked else None
                    q = taps_of(ext_q, filter_ref, 0, tile, ct, masks)
                    halves.append(q * y[pl.ds(pl.multiple_of(tile * 64 + ct * 8, 8), 8), :])
                both = jnp.concatenate(halves, axis=0).astype(jnp.bfloat16)
                gated_ref[pl.ds(pl.multiple_of(i * 16, 16), 16), pl.ds(ct * LANES, LANES)] = both

        near = any_between(firsts, base - 1, base + 16)

        @pl.when(near)
        def _():
            fill(True)

        @pl.when(jnp.logical_not(near))
        def _():
            fill(False)

        return 0

    lax.fori_loop(0, block_len // 16, gate_step, 0)
    part = jnp.dot(gated_ref[...], unembed_ref[...], preferred_element_type=jnp.float32)

    @pl.when(group == 0)
    def _():
        total[...] = part

    @pl.when(group > 0)
    def _():
        total[...] += part

    @pl.when(group == pl.num_programs(0) - 1)
    def _():
        logits_ref[...] = total[...].astype(jnp.bfloat16)


def loss_kernel(parts, logits_ref, target_ref, loss_ref, inbox, send_sem, recv_sem):
    me = lax.axis_index("chan")
    others = [lax.rem(me + d, parts) for d in range(1, parts)]
    greet([("chan", other, me >= 0) for other in others])
    copies = []
    for d in range(1, parts):
        copies.append(
            pltpu.make_async_remote_copy(
                src_ref=logits_ref,
                dst_ref=inbox.at[me],
                send_sem=send_sem.at[d - 1],
                recv_sem=recv_sem.at[d - 1],
                device_id={"chan": others[d - 1]},
                device_id_type=MESH,
            )
        )
        copies[-1].start()
    inbox[me] = logits_ref[...]
    for copy in copies:
        copy.wait_recv()
    block_len, vocab = logits_ref.shape
    eye = lax.broadcasted_iota(jnp.int32, (LANES, LANES), 0) == lax.broadcasted_iota(
        jnp.int32, (LANES, LANES), 1
    )
    vocab_ids = lax.broadcasted_iota(jnp.int32, (LANES, vocab), 1)
    for tile in range(block_len // LANES):
        rows = pl.ds(tile * LANES, LANES)
        logits = inbox[0, rows, :].astype(jnp.float32)
        for part in range(1, parts):
            logits = logits + inbox[part, rows, :].astype(jnp.float32)
        wanted = jnp.where(eye, target_ref[tile : tile + 1, :].astype(jnp.float32), 0.0)
        wanted = jnp.sum(wanted, axis=1, keepdims=True).astype(jnp.int32)
        peak = jnp.max(logits, axis=1, keepdims=True)
        exp_total = jnp.sum(jnp.exp(logits - peak), axis=1, keepdims=True)
        picked = jnp.sum(jnp.where(vocab_ids == wanted, logits, 0.0), axis=1, keepdims=True)
        loss = peak + jnp.log(exp_total) - picked
        loss_ref[tile : tile + 1, :] = jnp.sum(jnp.where(eye, loss, 0.0), axis=0, keepdims=True)
    for copy in copies:
        copy.wait_send()


def local(blocks, parts, streams, short_filter, pole_rates, residues, direct, doc_lengths, targets, unembed):
    block_len, chans = streams.shape[1], streams.shape[2]
    poles, vocab = pole_rates.shape[0], unembed.shape[1]
    groups = chans // GROUP
    f32, bf16 = jnp.float32, jnp.bfloat16
    shape = jax.ShapeDtypeStruct
    vmem = pl.BlockSpec(memory_space=pltpu.VMEM)
    smem = pl.BlockSpec(memory_space=pltpu.SMEM)
    params = functools.partial(pltpu.CompilerParams, vmem_limit_bytes=VMEM_LIMIT)

    edges = pl.pallas_call(
        functools.partial(edge_kernel, blocks),
        name="edges",
        grid=(1,),
        out_shape=shape((8, chans), f32),
        in_specs=[pl.BlockSpec((3, 16, chans), lambda g: (0, block_len // 16 - 1, 0))],
        out_specs=pl.BlockSpec((8, chans), lambda g: (0, 0)),
        scratch_shapes=[
            pltpu.VMEM((16, chans // 2), bf16),
            pltpu.VMEM((16, chans // 2), bf16),
            pltpu.SemaphoreType.DMA,
            pltpu.SemaphoreType.DMA,
        ],
        compiler_params=params(collective_id=0, has_side_effects=True),
    )(streams)

    def stream_spec(j):
        return pl.BlockSpec((1, block_len, GROUP), lambda g: (j, 0, g))

    edge_spec = pl.BlockSpec((8, GROUP), lambda g: (0, g))
    filter_spec = pl.BlockSpec((3, 3, GROUP), lambda g: (0, 0, g))
    pole_spec = pl.BlockSpec((poles, GROUP), lambda g: (0, g))
    turned_spec = pl.BlockSpec((poles, 1, 8, LANES), lambda g: (0, g, 0, 0))
    y_spec = pl.BlockSpec((1, block_len * 8, LANES), lambda g: (g, 0, 0))
    turned = shape((poles, groups, 8, LANES), f32)

    y_local, ends, rates, weights = pl.pallas_call(
        local_kernel,
        name="recur",
        grid=(groups,),
        out_shape=[shape((groups, block_len * 8, LANES), f32), turned, turned, turned],
        in_specs=[
            smem, stream_spec(1), stream_spec(2), edge_spec, filter_spec, pole_spec, pole_spec,
            pl.BlockSpec((1, GROUP), lambda g: (0, g)),
        ],
        out_specs=[y_spec, turned_spec, turned_spec, turned_spec],
        scratch_shapes=[
            pltpu.VMEM((8 * (block_len + 8), LANES), f32),
            pltpu.VMEM((8 * (block_len + 8), LANES), f32),
            pltpu.VMEM((poles * 8, LANES), f32),
            pltpu.VMEM((block_len * 8, LANES), f32),
        ],
        compiler_params=params(),
    )(doc_lengths, streams, streams, edges, short_filter, pole_rates, residues, direct.reshape(1, chans))

    rounds = max(1, (blocks - 1).bit_length())
    rows = poles * groups * 8
    pieces = 2
    incoming = pl.pallas_call(
        functools.partial(exchange_kernel, blocks, block_len, pieces),
        name="exchange",
        out_shape=shape((rows, LANES), f32),
        in_specs=[smem, vmem, vmem],
        out_specs=vmem,
        scratch_shapes=[
            pltpu.VMEM((rounds, rows, LANES), bf16),
            pltpu.VMEM((rounds, rows, LANES), bf16),
            pltpu.SemaphoreType.DMA((rounds, pieces)),
            pltpu.SemaphoreType.DMA((rounds, pieces)),
        ],
        compiler_params=params(collective_id=1, has_side_effects=True),
    )(doc_lengths, rates.reshape(rows, LANES), ends.reshape(rows, LANES))

    gated_out, logits = pl.pallas_call(
        finish_kernel,
        name="finish",
        grid=(groups,),
        out_shape=[shape((block_len, chans), bf16), shape((block_len, vocab), bf16)],
        in_specs=[
            smem, stream_spec(0), edge_spec, filter_spec, turned_spec, turned_spec, turned_spec, y_spec,
            pl.BlockSpec((GROUP, vocab), lambda g: (g, 0)),
        ],
        out_specs=[
            pl.BlockSpec((block_len, GROUP), lambda g: (0, g)),
            pl.BlockSpec((block_len, vocab), lambda g: (0, 0)),
        ],
        scratch_shapes=[
            pltpu.VMEM((8 * (block_len + 8), LANES), f32),
            pltpu.VMEM((block_len * 8, LANES), f32),
            pltpu.VMEM((block_len, vocab), f32),
        ],
        compiler_params=params(),
    )(
        doc_lengths, streams, edges, short_filter, rates, weights,
        incoming.reshape(turned.shape), y_local, unembed,
    )

    loss = pl.pallas_call(
        functools.partial(loss_kernel, parts),
        name="loss",
        out_shape=shape((block_len // LANES, LANES), f32),
        in_specs=[vmem, vmem],
        out_specs=vmem,
        scratch_shapes=[
            pltpu.VMEM((parts, block_len, vocab), bf16),
            pltpu.SemaphoreType.DMA((max(1, parts - 1),)),
            pltpu.SemaphoreType.DMA((max(1, parts - 1),)),
        ],
        compiler_params=params(collective_id=2, has_side_effects=True),
    )(logits, targets.reshape(block_len // LANES, LANES))
    return gated_out, loss.reshape(block_len)


def solution(mesh):
    in_specs = (
        P(None, "seq", "chan"),
        P(None, None, "chan"),
        P(None, "chan"),
        P(None, "chan"),
        P("chan"),
        P(),
        P("seq"),
        P("chan", None),
    )
    out_specs = (P("seq", "chan"), P("seq"))
    body = functools.partial(local, mesh.shape["seq"], mesh.shape["chan"])
    return jax.shard_map(body, mesh=mesh, in_specs=in_specs, out_specs=out_specs, check_vma=False)
```

```python
import functools

import jax
import jax.numpy as jnp
from jax import lax
from jax.experimental import pallas as pl
from jax.experimental.pallas import tpu as pltpu
from jax.sharding import PartitionSpec as P

MESH = pl.DeviceIdType.MESH
LANES = 128
GROUP = 8 * LANES
VMEM_LIMIT = 48 * 1024 * 1024


def doc_firsts(lengths_ref):
    firsts = [jnp.int32(0)]
    for d in range(lengths_ref.shape[0] - 1):
        firsts.append(firsts[-1] + lengths_ref[d])
    return firsts


def any_between(firsts, low, high):
    found = jnp.bool_(False)
    for first in firsts:
        found = found | ((first >= low) & (first < high))
    return found


def greet(peers):
    barrier = pltpu.get_barrier_semaphore()
    for axis, peer, there in peers:

        @pl.when(there)
        def _():
            pl.semaphore_signal(barrier, inc=1, device_id={axis: peer}, device_id_type=MESH)

    if peers:
        pl.semaphore_wait(barrier, sum(jnp.where(there, 1, 0) for _, _, there in peers))


def edge_kernel(blocks, tail_ref, out_ref, packed, landed, send_sem, recv_sem):
    me = lax.axis_index("seq")
    half = packed.shape[1]
    greet((("seq", me + 1, me < blocks - 1), ("seq", me - 1, me > 0)))
    rows = []
    for side in range(2):
        cols = pl.ds(side * half, half)
        for j in range(3):
            rows.append(tail_ref[j, :, cols].astype(jnp.float32)[14:16])
        rows.append(jnp.zeros((2, half), jnp.float32))
    packed[...] = jnp.concatenate(rows, axis=0).astype(jnp.bfloat16)
    copy = pltpu.make_async_remote_copy(
        src_ref=packed,
        dst_ref=landed,
        send_sem=send_sem,
        recv_sem=recv_sem,
        device_id={"seq": me + 1},
        device_id_type=MESH,
    )

    @pl.when(me < blocks - 1)
    def _():
        copy.start()

    @pl.when(me > 0)
    def _():
        copy.wait_recv()
        got = landed[...].astype(jnp.float32)
        out_ref[:, pl.ds(0, half)] = got[0:8]
        out_ref[:, pl.ds(half, half)] = got[8:16]

    @pl.when(me == 0)
    def _():
        out_ref[...] = jnp.zeros_like(out_ref)

    @pl.when(me < blocks - 1)
    def _():
        copy.wait_send()


def load_extended(ext, stream_ref, edge_ref, stream_id):
    block_len = stream_ref.shape[1]
    pitch = block_len + 8
    for ct in range(8):
        edge = edge_ref[:, pl.ds(ct * LANES, LANES)]
        both = jnp.concatenate([edge[0:6], edge[2 * stream_id : 2 * stream_id + 2]], axis=0)
        ext[pl.ds(ct * pitch, 8), :] = both

    def step(i, _):
        rows = pl.ds(pl.multiple_of(i * 16, 16), 16)
        for ct in range(8):
            tile = stream_ref[0, rows, pl.ds(ct * LANES, LANES)].astype(jnp.float32)
            ext[pl.ds(pl.multiple_of(ct * pitch + i * 16 + 8, 8), 16), :] = tile
        return 0

    lax.fori_loop(0, block_len // 16, step, 0)


def load_taps(filter_ref, stream_id, ct):
    cols = pl.ds(ct * LANES, LANES)
    return [
        jnp.broadcast_to(filter_ref[stream_id, shift : shift + 1, cols], (8, LANES)) for shift in range(3)
    ]


def filter_tile(ext, taps, i, ct, masks=None):
    pitch = ext.shape[0] // 8
    terms = []
    for shift in range(3):
        term = taps[shift] * ext[pl.ds(ct * pitch + i * 8 + (8 - shift), 8), :]
        if shift and masks is not None:
            term = jnp.where(masks[shift - 1], term, 0.0)
        terms.append(term)
    return terms[0] + terms[1] + terms[2]


def at_starts(firsts, first_pos, block_len, tile_len, redo):
    for first in firsts:
        for after in range(2):
            place = first + after - first_pos

            @pl.when((place >= 0) & (place < block_len))
            def _():
                redo(place // tile_len)


def tile_masks(firsts, base):
    pos = base + lax.broadcasted_iota(jnp.int32, (8, LANES), 0)
    start = jnp.zeros((8, LANES), jnp.int32)
    for first in firsts:
        start = jnp.maximum(start, jnp.where(first <= pos, first, 0))
    return [pos - shift >= start for shift in (1, 2)]


def to_sublanes(ref, scratch, row_count):
    for top in range(0, row_count, 8):
        for ct in range(8):
            scratch[pl.ds(top * 8 + ct * 8, 8), :] = ref[top : top + 8, pl.ds(ct * LANES, LANES)]
    return [scratch[pl.ds((p // 8) * 64 + p % 8, 8, stride=8), :] for p in range(row_count)]


def local_kernel(
    lengths_ref, k_ref, v_ref, edge_ref, filter_ref, rate_ref, residue_ref, direct_ref,
    y_ref, end_ref, rate_out, weight_out,
    ext_k, ext_v, turn, driver,
):
    block_len = k_ref.shape[1]
    poles = rate_ref.shape[0]
    first_pos = lax.axis_index("seq") * block_len
    firsts = doc_firsts(lengths_ref)
    load_extended(ext_k, k_ref, edge_ref, 1)
    load_extended(ext_v, v_ref, edge_ref, 2)

    for ct in range(8):
        k_taps = load_taps(filter_ref, 1, ct)
        v_taps = load_taps(filter_ref, 2, ct)

        def filter_step(i, _):
            k = filter_tile(ext_k, k_taps, i, ct)
            v = filter_tile(ext_v, v_taps, i, ct)
            driver[pl.ds(pl.multiple_of(i * 64 + ct * 8, 8), 8), :] = k * v
            return 0

        lax.fori_loop(0, block_len // 8, filter_step, 0, unroll=8)

    def refilter(i):
        masks = tile_masks(firsts, first_pos + i * 8)
        for ct in range(8):
            k = filter_tile(ext_k, load_taps(filter_ref, 1, ct), i, ct, masks)
            v = filter_tile(ext_v, load_taps(filter_ref, 2, ct), i, ct, masks)
            driver[pl.ds(pl.multiple_of(i * 64 + ct * 8, 8), 8), :] = k * v

    at_starts(firsts, first_pos, block_len, 8, refilter)

    rates = to_sublanes(rate_ref, turn, poles)
    decays = [jnp.exp(-r) for r in rates]
    for p in range(poles):
        rate_out[p, 0] = rates[p]
    residues = to_sublanes(residue_ref, turn, poles)
    weights = [residues[p] * (1.0 - decays[p]) for p in range(poles)]
    for p in range(poles):
        weight_out[p, 0] = weights[p]
    for ct in range(8):
        turn[pl.ds(ct * 8, 8), :] = jnp.broadcast_to(direct_ref[:, pl.ds(ct * LANES, LANES)], (8, LANES))
    direct = turn[pl.ds(0, 8, stride=8), :]

    def chunk(i, states):
        base = first_pos + i * 8

        def run(states, with_reset):
            states = list(states)
            for j in range(8):
                x = driver[pl.ds(i * 64 + j, 8, stride=8), :]
                if with_reset:
                    hit = any_between(firsts, base + j, base + j + 1)
                    keep = jnp.where(hit, 0.0, 1.0)
                sums = [direct * x, None, None, None]
                for p in range(poles):
                    held = states[p] * keep if with_reset else states[p]
                    states[p] = decays[p] * held + x
                    term = weights[p] * states[p]
                    sums[p % 4] = term if sums[p % 4] is None else sums[p % 4] + term
                y_ref[0, pl.ds(i * 64 + j, 8, stride=8), :] = (sums[0] + sums[1]) + (sums[2] + sums[3])
            return tuple(states)

        return lax.cond(
            any_between(firsts, base, base + 8),
            lambda s: run(s, True),
            lambda s: run(s, False),
            states,
        )

    zeros = tuple(jnp.zeros((8, LANES), jnp.float32) for _ in range(poles))
    states = lax.fori_loop(0, block_len // 8, chunk, zeros)
    for p in range(poles):
        end_ref[p, 0] = states[p]


def exchange_kernel(blocks, block_len, pieces, lengths_ref, rate_ref, end_ref, in_ref, outbox, inbox, send_sem, recv_sem):
    me = lax.axis_index("seq")
    first_pos = me * block_len
    rounds = max(1, (blocks - 1).bit_length())
    peers = []
    for k in range(rounds):
        peers.append(("seq", me + (1 << k), me + (1 << k) < blocks))
        peers.append(("seq", me - (1 << k), me >= (1 << k)))
    greet(peers)
    firsts = doc_firsts(lengths_ref)

    def last_start(pos):
        best = jnp.int32(0)
        for first in firsts:
            best = jnp.maximum(best, jnp.where(first <= pos, first, 0))
        return best

    own_keep = jnp.where(last_start(first_pos + block_len - 1) < first_pos, 1.0, 0.0)
    span = end_ref.shape[0] // pieces

    def copy(k, piece):
        rows = pl.ds(piece * span, span)
        return pltpu.make_async_remote_copy(
            src_ref=outbox.at[k, rows],
            dst_ref=inbox.at[k, rows],
            send_sem=send_sem.at[k, piece],
            recv_sem=recv_sem.at[k, piece],
            device_id={"seq": me + (1 << k)},
            device_id_type=MESH,
        )

    in_ref[...] = jnp.zeros_like(in_ref)

    def send(k, piece):
        rows = pl.ds(piece * span, span)

        @pl.when(me + (1 << k) < blocks)
        def _():
            whole = end_ref[rows, :]
            if k:
                fade = jnp.exp(-rate_ref[rows, :] * float(block_len)) * own_keep
                whole = whole + fade * in_ref[rows, :]
            outbox[k, rows, :] = whole.astype(jnp.bfloat16)
            copy(k, piece).start()

    def receive(k, piece):
        rows = pl.ds(piece * span, span)
        reach = 1 << k
        far = first_pos - (reach - 1) * block_len

        @pl.when(me >= reach)
        def _():
            copy(k, piece).wait_recv()
            got = inbox[k, rows, :].astype(jnp.float32)
            if k:
                clear = jnp.where(last_start(first_pos - 1) < far, 1.0, 0.0)
                got = got * (jnp.exp(-rate_ref[rows, :] * float((reach - 1) * block_len)) * clear)
            in_ref[rows, :] += got

    for piece in range(pieces):
        send(0, piece)
    for k in range(rounds):
        for piece in range(pieces):
            receive(k, piece)
            if k + 1 < rounds:
                send(k + 1, piece)

    for k in range(rounds):
        for piece in range(pieces):

            @pl.when(me + (1 << k) < blocks)
            def _():
                copy(k, piece).wait_send()


def finish_kernel(
    lengths_ref, q_ref, edge_ref, filter_ref, rate_ref, weight_ref, in_ref, y_in, unembed_ref,
    gated_ref, logits_ref,
    ext_q, y, total,
):
    block_len = q_ref.shape[1]
    poles = rate_ref.shape[0]
    first_pos = lax.axis_index("seq") * block_len
    firsts = doc_firsts(lengths_ref)
    group = pl.program_id(0)
    cut = jnp.int32(block_len)
    for first in firsts:
        cut = jnp.where(first >= first_pos, jnp.minimum(cut, first - first_pos), cut)
    load_extended(ext_q, q_ref, edge_ref, 0)
    decays = [jnp.exp(-rate_ref[p, 0]) for p in range(poles)]
    fading = tuple(weight_ref[p, 0] * in_ref[p, 0] * decays[p] for p in range(poles))

    def fade_chunk(i, fading):
        fading = list(fading)
        for j in range(8):
            sums = [fading[0], fading[1], fading[2], fading[3]]
            for p in range(4, poles):
                sums[p % 4] = sums[p % 4] + fading[p]
            arrived = (sums[0] + sums[1]) + (sums[2] + sums[3])
            rows = pl.ds(i * 64 + j, 8, stride=8)
            y[rows, :] = jnp.where(i * 8 + j < cut, 1.0, 0.0) * arrived
            fading = [f * d for f, d in zip(fading, decays)]
        return tuple(fading)

    carried = (cut + 7) // 8
    lax.fori_loop(0, carried, fade_chunk, fading)

    def plain_chunk(i, _):
        rows = pl.ds(pl.multiple_of(i * 64, 64), 64)
        y[rows, :] = jnp.zeros((64, LANES), jnp.float32)
        return 0

    lax.fori_loop(carried, block_len // 8, plain_chunk, 0)

    def gate(i, ct, taps, masks):
        halves = []
        for side in range(2):
            tile = i * 2 + side
            q = filter_tile(ext_q, taps, tile, ct, masks[side])
            rows = pl.ds(pl.multiple_of(tile * 64 + ct * 8, 8), 8)
            halves.append(q * (y_in[0, rows, :] + y[rows, :]))
        both = jnp.concatenate(halves, axis=0).astype(jnp.bfloat16)
        gated_ref[pl.ds(pl.multiple_of(i * 16, 16), 16), pl.ds(ct * LANES, LANES)] = both

    for ct in range(8):
        taps = load_taps(filter_ref, 0, ct)

        def gate_step(i, _):
            gate(i, ct, taps, [None, None])
            return 0

        lax.fori_loop(0, block_len // 16, gate_step, 0, unroll=4)

    def regate(i):
        masks = [tile_masks(firsts, first_pos + i * 16 + side * 8) for side in range(2)]
        for ct in range(8):
            gate(i, ct, load_taps(filter_ref, 0, ct), masks)

    at_starts(firsts, first_pos, block_len, 16, regate)
    part = jnp.dot(gated_ref[...], unembed_ref[...], preferred_element_type=jnp.float32)

    @pl.when(group == 0)
    def _():
        total[...] = part

    @pl.when(group > 0)
    def _():
        total[...] += part

    @pl.when(group == pl.num_programs(0) - 1)
    def _():
        logits_ref[...] = total[...].astype(jnp.bfloat16)


def loss_kernel(parts, logits_ref, target_ref, loss_ref, inbox, send_sem, recv_sem):
    me = lax.axis_index("chan")
    others = [lax.rem(me + d, parts) for d in range(1, parts)]
    greet([("chan", other, me >= 0) for other in others])
    copies = []
    for d in range(1, parts):
        copies.append(
            pltpu.make_async_remote_copy(
                src_ref=logits_ref,
                dst_ref=inbox.at[me],
                send_sem=send_sem.at[d - 1],
                recv_sem=recv_sem.at[d - 1],
                device_id={"chan": others[d - 1]},
                device_id_type=MESH,
            )
        )
        copies[-1].start()
    inbox[me] = logits_ref[...]
    for copy in copies:
        copy.wait_recv()
    block_len, vocab = logits_ref.shape
    eye = lax.broadcasted_iota(jnp.int32, (LANES, LANES), 0) == lax.broadcasted_iota(
        jnp.int32, (LANES, LANES), 1
    )
    vocab_ids = lax.broadcasted_iota(jnp.int32, (LANES, vocab), 1)
    for tile in range(block_len // LANES):
        rows = pl.ds(tile * LANES, LANES)
        logits = inbox[0, rows, :].astype(jnp.float32)
        for part in range(1, parts):
            logits = logits + inbox[part, rows, :].astype(jnp.float32)
        wanted = jnp.where(eye, target_ref[tile : tile + 1, :].astype(jnp.float32), 0.0)
        wanted = jnp.sum(wanted, axis=1, keepdims=True).astype(jnp.int32)
        peak = jnp.max(logits, axis=1, keepdims=True)
        exp_total = jnp.sum(jnp.exp(logits - peak), axis=1, keepdims=True)
        picked = jnp.sum(jnp.where(vocab_ids == wanted, logits, 0.0), axis=1, keepdims=True)
        loss = peak + jnp.log(exp_total) - picked
        loss_ref[tile : tile + 1, :] = jnp.sum(jnp.where(eye, loss, 0.0), axis=0, keepdims=True)
    for copy in copies:
        copy.wait_send()


def local(blocks, parts, streams, short_filter, pole_rates, residues, direct, doc_lengths, targets, unembed):
    block_len, chans = streams.shape[1], streams.shape[2]
    poles, vocab = pole_rates.shape[0], unembed.shape[1]
    groups = chans // GROUP
    f32, bf16 = jnp.float32, jnp.bfloat16
    shape = jax.ShapeDtypeStruct
    vmem = pl.BlockSpec(memory_space=pltpu.VMEM)
    smem = pl.BlockSpec(memory_space=pltpu.SMEM)
    params = functools.partial(pltpu.CompilerParams, vmem_limit_bytes=VMEM_LIMIT)

    edges = pl.pallas_call(
        functools.partial(edge_kernel, blocks),
        name="edges",
        grid=(1,),
        out_shape=shape((8, chans), f32),
        in_specs=[pl.BlockSpec((3, 16, chans), lambda g: (0, block_len // 16 - 1, 0))],
        out_specs=pl.BlockSpec((8, chans), lambda g: (0, 0)),
        scratch_shapes=[
            pltpu.VMEM((16, chans // 2), bf16),
            pltpu.VMEM((16, chans // 2), bf16),
            pltpu.SemaphoreType.DMA,
            pltpu.SemaphoreType.DMA,
        ],
        compiler_params=params(collective_id=0, has_side_effects=True),
    )(streams)

    def stream_spec(j):
        return pl.BlockSpec((1, block_len, GROUP), lambda g: (j, 0, g))

    edge_spec = pl.BlockSpec((8, GROUP), lambda g: (0, g))
    filter_spec = pl.BlockSpec((3, 3, GROUP), lambda g: (0, 0, g))
    pole_spec = pl.BlockSpec((poles, GROUP), lambda g: (0, g))
    turned_spec = pl.BlockSpec((poles, 1, 8, LANES), lambda g: (0, g, 0, 0))
    y_spec = pl.BlockSpec((1, block_len * 8, LANES), lambda g: (g, 0, 0))
    turned = shape((poles, groups, 8, LANES), f32)

    y_local, ends, rates, weights = pl.pallas_call(
        local_kernel,
        name="recur",
        grid=(groups,),
        out_shape=[shape((groups, block_len * 8, LANES), f32), turned, turned, turned],
        in_specs=[
            smem, stream_spec(1), stream_spec(2), edge_spec, filter_spec, pole_spec, pole_spec,
            pl.BlockSpec((1, GROUP), lambda g: (0, g)),
        ],
        out_specs=[y_spec, turned_spec, turned_spec, turned_spec],
        scratch_shapes=[
            pltpu.VMEM((8 * (block_len + 8), LANES), f32),
            pltpu.VMEM((8 * (block_len + 8), LANES), f32),
            pltpu.VMEM((poles * 8, LANES), f32),
            pltpu.VMEM((block_len * 8, LANES), f32),
        ],
        compiler_params=params(),
    )(doc_lengths, streams, streams, edges, short_filter, pole_rates, residues, direct.reshape(1, chans))

    rounds = max(1, (blocks - 1).bit_length())
    rows = poles * groups * 8
    pieces = 4
    incoming = pl.pallas_call(
        functools.partial(exchange_kernel, blocks, block_len, pieces),
        name="exchange",
        out_shape=shape((rows, LANES), f32),
        in_specs=[smem, vmem, vmem],
        out_specs=vmem,
        scratch_shapes=[
            pltpu.VMEM((rounds, rows, LANES), bf16),
            pltpu.VMEM((rounds, rows, LANES), bf16),
            pltpu.SemaphoreType.DMA((rounds, pieces)),
            pltpu.SemaphoreType.DMA((rounds, pieces)),
        ],
        compiler_params=params(collective_id=1, has_side_effects=True),
    )(doc_lengths, rates.reshape(rows, LANES), ends.reshape(rows, LANES))

    gated_out, logits = pl.pallas_call(
        finish_kernel,
        name="finish",
        grid=(groups,),
        out_shape=[shape((block_len, chans), bf16), shape((block_len, vocab), bf16)],
        in_specs=[
            smem, stream_spec(0), edge_spec, filter_spec, turned_spec, turned_spec, turned_spec, y_spec,
            pl.BlockSpec((GROUP, vocab), lambda g: (g, 0)),
        ],
        out_specs=[
            pl.BlockSpec((block_len, GROUP), lambda g: (0, g)),
            pl.BlockSpec((block_len, vocab), lambda g: (0, 0)),
        ],
        scratch_shapes=[
            pltpu.VMEM((8 * (block_len + 8), LANES), f32),
            pltpu.VMEM((block_len * 8, LANES), f32),
            pltpu.VMEM((block_len, vocab), f32),
        ],
        compiler_params=params(),
    )(
        doc_lengths, streams, edges, short_filter, rates, weights,
        incoming.reshape(turned.shape), y_local, unembed,
    )

    loss = pl.pallas_call(
        functools.partial(loss_kernel, parts),
        name="loss",
        out_shape=shape((block_len // LANES, LANES), f32),
        in_specs=[vmem, vmem],
        out_specs=vmem,
        scratch_shapes=[
            pltpu.VMEM((parts, block_len, vocab), bf16),
            pltpu.SemaphoreType.DMA((max(1, parts - 1),)),
            pltpu.SemaphoreType.DMA((max(1, parts - 1),)),
        ],
        compiler_params=params(collective_id=2, has_side_effects=True),
    )(logits, targets.reshape(block_len // LANES, LANES))
    return gated_out, loss.reshape(block_len)


def solution(mesh):
    in_specs = (
        P(None, "seq", "chan"),
        P(None, None, "chan"),
        P(None, "chan"),
        P(None, "chan"),
        P("chan"),
        P(),
        P("seq"),
        P("chan", None),
    )
    out_specs = (P("seq", "chan"), P("seq"))
    body = functools.partial(local, mesh.shape["seq"], mesh.shape["chan"])
    return jax.shard_map(body, mesh=mesh, in_specs=in_specs, out_specs=out_specs, check_vma=False)
```

```python
import functools

import jax
import jax.numpy as jnp
from jax import lax
from jax.experimental import pallas as pl
from jax.experimental.pallas import tpu as pltpu
from jax.sharding import PartitionSpec as P

MESH = pl.DeviceIdType.MESH
LANES = 128
GROUP = 8 * LANES
VMEM_LIMIT = 48 * 1024 * 1024


def doc_firsts(lengths_ref):
    firsts = [jnp.int32(0)]
    for d in range(lengths_ref.shape[0] - 1):
        firsts.append(firsts[-1] + lengths_ref[d])
    return firsts


def any_between(firsts, low, high):
    found = jnp.bool_(False)
    for first in firsts:
        found = found | ((first >= low) & (first < high))
    return found


def greet(peers):
    barrier = pltpu.get_barrier_semaphore()
    for axis, peer, there in peers:

        @pl.when(there)
        def _():
            pl.semaphore_signal(barrier, inc=1, device_id={axis: peer}, device_id_type=MESH)

    if peers:
        pl.semaphore_wait(barrier, sum(jnp.where(there, 1, 0) for _, _, there in peers))


def load_edge(ext, edge_ref, stream_id, first_col=0):
    pitch = ext.shape[0] // 8
    for ct in range(8):
        edge = edge_ref[:, pl.ds(first_col + ct * LANES, LANES)]
        both = jnp.concatenate([edge[0:6], edge[2 * stream_id : 2 * stream_id + 2]], axis=0)
        ext[pl.ds(ct * pitch, 8), :] = both


def load_block(ext, stream_ref):
    block_len = stream_ref.shape[1]
    pitch = block_len + 8

    def step(i, _):
        rows = pl.ds(pl.multiple_of(i * 16, 16), 16)
        for ct in range(8):
            tile = stream_ref[0, rows, pl.ds(ct * LANES, LANES)].astype(jnp.float32)
            ext[pl.ds(pl.multiple_of(ct * pitch + i * 16 + 8, 8), 16), :] = tile
        return 0

    lax.fori_loop(0, block_len // 16, step, 0)


def load_taps(filter_ref, stream_id, ct):
    cols = pl.ds(ct * LANES, LANES)
    return [
        jnp.broadcast_to(filter_ref[stream_id, shift : shift + 1, cols], (8, LANES)) for shift in range(3)
    ]


def filter_tile(ext, taps, i, ct, masks=None):
    pitch = ext.shape[0] // 8
    terms = []
    for shift in range(3):
        term = taps[shift] * ext[pl.ds(ct * pitch + i * 8 + (8 - shift), 8), :]
        if shift and masks is not None:
            term = term * masks[shift - 1]
        terms.append(term)
    return terms[0] + terms[1] + terms[2]


def at_starts(firsts, first_pos, block_len, tile_len, redo):
    for first in firsts:
        for after in range(2):
            place = first + after - first_pos

            @pl.when((place >= 0) & (place < block_len))
            def _():
                redo(place // tile_len)


def tile_masks(firsts, base):
    pos = base + lax.broadcasted_iota(jnp.int32, (8, LANES), 0)
    start = jnp.zeros((8, LANES), jnp.int32)
    for first in firsts:
        start = jnp.maximum(start, jnp.where(first <= pos, first, 0))
    return [pos - shift >= start for shift in (1, 2)]


def to_sublanes(ref, scratch, row_count):
    for top in range(0, row_count, 8):
        for ct in range(8):
            scratch[pl.ds(top * 8 + ct * 8, 8), :] = ref[top : top + 8, pl.ds(ct * LANES, LANES)]
    return [scratch[pl.ds((p // 8) * 64 + p % 8, 8, stride=8), :] for p in range(row_count)]


def recur_kernel(
    blocks, groups,
    lengths_ref, tail_ref, k_ref, v_ref, filter_ref, rate_ref, residue_ref, direct_ref,
    y_ref, edge_ref, rate_out, weight_out, in_ref,
    ext_k, ext_v, turn, driver, mask_1, mask_2, table, ends,
    packed, landed, outbox, inbox, edge_send, edge_recv, send_sem, recv_sem,
):
    block_len = k_ref.shape[1]
    poles = rate_ref.shape[0]
    span = poles * 8
    group = pl.program_id(0)
    me = lax.axis_index("seq")
    first_pos = me * block_len
    firsts = doc_firsts(lengths_ref)
    rounds = max(1, (blocks - 1).bit_length())
    half = packed.shape[1]

    def last_start(pos):
        best = jnp.int32(0)
        for first in firsts:
            best = jnp.maximum(best, jnp.where(first <= pos, first, 0))
        return best

    edge_copy = pltpu.make_async_remote_copy(
        src_ref=packed,
        dst_ref=landed,
        send_sem=edge_send,
        recv_sem=edge_recv,
        device_id={"seq": me + 1},
        device_id_type=MESH,
    )

    def state_copy(k, piece):
        rows = pl.ds(pl.multiple_of(piece * span, span), span)
        return pltpu.make_async_remote_copy(
            src_ref=outbox.at[k, rows],
            dst_ref=inbox.at[k, rows],
            send_sem=send_sem.at[k, piece],
            recv_sem=recv_sem.at[k, piece],
            device_id={"seq": me + (1 << k)},
            device_id_type=MESH,
        )

    own_keep = jnp.where(last_start(first_pos + block_len - 1) < first_pos, 1.0, 0.0)

    def send(k, piece):
        rows = pl.ds(pl.multiple_of(piece * span, span), span)

        @pl.when(me + (1 << k) < blocks)
        def _():
            whole = ends[rows, :]
            if k:
                fade = jnp.exp(-rate_out[rows, :] * float(block_len)) * own_keep
                whole = whole + fade * in_ref[rows, :]
            outbox[k, rows, :] = whole.astype(jnp.bfloat16)
            state_copy(k, piece).start()

    def receive(k, piece):
        rows = pl.ds(pl.multiple_of(piece * span, span), span)
        reach = 1 << k
        far = first_pos - (reach - 1) * block_len

        @pl.when(me >= reach)
        def _():
            state_copy(k, piece).wait_recv()
            got = inbox[k, rows, :].astype(jnp.float32)
            if k:
                clear = jnp.where(last_start(first_pos - 1) < far, 1.0, 0.0)
                got = got * (jnp.exp(-rate_out[rows, :] * float((reach - 1) * block_len)) * clear)
            in_ref[rows, :] += got

    def relay(k, piece):
        receive(k, piece)
        if k + 1 < rounds:
            send(k + 1, piece)

    @pl.when(group == 0)
    def _():
        rows = []
        for side in range(2):
            cols = pl.ds(side * half, half)
            for j in range(3):
                rows.append(tail_ref[j, :, cols].astype(jnp.float32)[14:16])
            rows.append(jnp.zeros((2, half), jnp.float32))
        packed[...] = jnp.concatenate(rows, axis=0).astype(jnp.bfloat16)
        peers = []
        for k in range(rounds):
            peers.append(("seq", me + (1 << k), me + (1 << k) < blocks))
            peers.append(("seq", me - (1 << k), me >= (1 << k)))
        greet(peers)

        @pl.when(me < blocks - 1)
        def _():
            edge_copy.start()

        in_ref[...] = jnp.zeros_like(in_ref)
        table[pl.ds(span, span), :] = jnp.zeros((span, LANES), jnp.float32)
        for i in range(block_len // 8):
            masks = tile_masks(firsts, first_pos + i * 8)
            mask_1[pl.ds(i * 8, 8), :] = jnp.where(masks[0], 1.0, 0.0)
            mask_2[pl.ds(i * 8, 8), :] = jnp.where(masks[1], 1.0, 0.0)

    load_block(ext_k, k_ref)
    load_block(ext_v, v_ref)

    rates = to_sublanes(rate_ref, turn, poles)
    decays = [jnp.exp(-r) for r in rates]
    own = pl.multiple_of(group * span, span)
    for p in range(poles):
        rate_out[pl.ds(own + p * 8, 8), :] = rates[p]
        table[pl.ds(p * 8, 8), :] = decays[p]
    residues = to_sublanes(residue_ref, turn, poles)
    weights = [residues[p] * (1.0 - decays[p]) for p in range(poles)]
    for p in range(poles):
        weight_out[pl.ds(own + p * 8, 8), :] = weights[p]
    for ct in range(8):
        turn[pl.ds(ct * 8, 8), :] = jnp.broadcast_to(direct_ref[:, pl.ds(ct * LANES, LANES)], (8, LANES))
    direct = turn[pl.ds(0, 8, stride=8), :]

    @pl.when(group == 0)
    def _():
        @pl.when(me > 0)
        def _():
            edge_copy.wait_recv()
            got = landed[...].astype(jnp.float32)
            edge_ref[:, pl.ds(0, half)] = got[0:8]
            edge_ref[:, pl.ds(half, half)] = got[8:16]

        @pl.when(me == 0)
        def _():
            edge_ref[...] = jnp.zeros_like(edge_ref)

    first_col = pl.multiple_of(group * GROUP, GROUP)
    load_edge(ext_k, edge_ref, 1, first_col)
    load_edge(ext_v, edge_ref, 2, first_col)

    for ct in range(8):
        k_taps = load_taps(filter_ref, 1, ct)
        v_taps = load_taps(filter_ref, 2, ct)

        def filter_step(i, _):
            rows = pl.ds(pl.multiple_of(i * 8, 8), 8)
            masks = (mask_1[rows, :], mask_2[rows, :])
            k = filter_tile(ext_k, k_taps, i, ct, masks)
            v = filter_tile(ext_v, v_taps, i, ct, masks)
            driver[pl.ds(pl.multiple_of(i * 64 + ct * 8, 8), 8), :] = k * v
            return 0

        lax.fori_loop(0, block_len // 8, filter_step, 0, unroll=8)

    def chunk(i, states):
        states = list(states)
        for j in range(8):
            x = driver[pl.ds(i * 64 + j, 8, stride=8), :]
            place = first_pos + i * 8 + j
            bank = jnp.where(any_between(firsts, place, place + 1), span, 0)
            sums = [direct * x, None, None, None]
            for p in range(poles):
                states[p] = table[pl.ds(bank + p * 8, 8), :] * states[p] + x
                term = weights[p] * states[p]
                sums[p % 4] = term if sums[p % 4] is None else sums[p % 4] + term
            y_ref[0, pl.ds(i * 64 + j, 8, stride=8), :] = (sums[0] + sums[1]) + (sums[2] + sums[3])
        return tuple(states)

    chunks = block_len // 8
    states = tuple(jnp.zeros((8, LANES), jnp.float32) for _ in range(poles))
    states = lax.fori_loop(0, chunks // 2, chunk, states)
    for k in range(0, rounds, 2):
        piece = group - 1 - k // 2

        @pl.when(piece >= 0)
        def _():
            relay(k, piece)

    states = lax.fori_loop(chunks // 2, chunks, chunk, states)
    for p in range(poles):
        ends[pl.ds(own + p * 8, 8), :] = states[p]
    send(0, group)
    for k in range(1, rounds, 2):
        piece = group - (k + 1) // 2

        @pl.when(piece >= 0)
        def _():
            relay(k, piece)

    @pl.when(group == groups - 1)
    def _():
        for slot in range(2 * groups, 2 * groups + rounds):
            for k in reversed(range(rounds)):
                piece, odd = divmod(slot - 2 - k, 2)
                if odd == 0 and 0 <= piece < groups:
                    relay(k, piece)
        for k in range(rounds):
            for piece in range(groups):

                @pl.when(me + (1 << k) < blocks)
                def _():
                    state_copy(k, piece).wait_send()

        @pl.when(me < blocks - 1)
        def _():
            edge_copy.wait_send()


def finish_kernel(
    lengths_ref, q_ref, edge_ref, filter_ref, rate_ref, weight_ref, in_ref, y_in, unembed_ref,
    gated_ref, logits_ref,
    ext_q, y, total,
):
    block_len = q_ref.shape[1]
    poles = rate_ref.shape[0] // 8
    first_pos = lax.axis_index("seq") * block_len
    firsts = doc_firsts(lengths_ref)
    group = pl.program_id(0)
    cut = jnp.int32(block_len)
    for first in firsts:
        cut = jnp.where(first >= first_pos, jnp.minimum(cut, first - first_pos), cut)
    load_block(ext_q, q_ref)
    load_edge(ext_q, edge_ref, 0)
    tiles = [pl.ds(p * 8, 8) for p in range(poles)]
    decays = [jnp.exp(-rate_ref[tile, :]) for tile in tiles]
    fading = tuple(weight_ref[tile, :] * in_ref[tile, :] * d for tile, d in zip(tiles, decays))

    def fade_chunk(i, fading):
        fading = list(fading)
        for j in range(8):
            sums = [fading[0], fading[1], fading[2], fading[3]]
            for p in range(4, poles):
                sums[p % 4] = sums[p % 4] + fading[p]
            arrived = (sums[0] + sums[1]) + (sums[2] + sums[3])
            rows = pl.ds(i * 64 + j, 8, stride=8)
            y[rows, :] = jnp.where(i * 8 + j < cut, 1.0, 0.0) * arrived
            fading = [f * d for f, d in zip(fading, decays)]
        return tuple(fading)

    carried = (cut + 7) // 8
    lax.fori_loop(0, carried, fade_chunk, fading)

    def plain_chunk(i, _):
        rows = pl.ds(pl.multiple_of(i * 64, 64), 64)
        y[rows, :] = jnp.zeros((64, LANES), jnp.float32)
        return 0

    lax.fori_loop(carried, block_len // 8, plain_chunk, 0)

    def gate(i, ct, taps, masks):
        halves = []
        for side in range(2):
            tile = i * 2 + side
            q = filter_tile(ext_q, taps, tile, ct, masks[side])
            rows = pl.ds(pl.multiple_of(tile * 64 + ct * 8, 8), 8)
            halves.append(q * (y_in[0, rows, :] + y[rows, :]))
        both = jnp.concatenate(halves, axis=0).astype(jnp.bfloat16)
        gated_ref[pl.ds(pl.multiple_of(i * 16, 16), 16), pl.ds(ct * LANES, LANES)] = both

    for ct in range(8):
        taps = load_taps(filter_ref, 0, ct)

        def gate_step(i, _):
            gate(i, ct, taps, [None, None])
            return 0

        lax.fori_loop(0, block_len // 16, gate_step, 0, unroll=4)

    def regate(i):
        masks = []
        for side in range(2):
            pair = tile_masks(firsts, first_pos + i * 16 + side * 8)
            masks.append([jnp.where(m, 1.0, 0.0) for m in pair])
        for ct in range(8):
            gate(i, ct, load_taps(filter_ref, 0, ct), masks)

    at_starts(firsts, first_pos, block_len, 16, regate)
    part = jnp.dot(gated_ref[...], unembed_ref[...], preferred_element_type=jnp.float32)

    @pl.when(group == 0)
    def _():
        total[...] = part

    @pl.when(group > 0)
    def _():
        total[...] += part

    @pl.when(group == pl.num_programs(0) - 1)
    def _():
        logits_ref[...] = total[...].astype(jnp.bfloat16)


def loss_kernel(parts, logits_ref, target_ref, loss_ref, inbox, send_sem, recv_sem):
    me = lax.axis_index("chan")
    others = [lax.rem(me + d, parts) for d in range(1, parts)]
    greet([("chan", other, me >= 0) for other in others])
    copies = []
    for d in range(1, parts):
        copies.append(
            pltpu.make_async_remote_copy(
                src_ref=logits_ref,
                dst_ref=inbox.at[me],
                send_sem=send_sem.at[d - 1],
                recv_sem=recv_sem.at[d - 1],
                device_id={"chan": others[d - 1]},
                device_id_type=MESH,
            )
        )
        copies[-1].start()
    inbox[me] = logits_ref[...]
    for copy in copies:
        copy.wait_recv()
    block_len, vocab = logits_ref.shape
    eye = lax.broadcasted_iota(jnp.int32, (LANES, LANES), 0) == lax.broadcasted_iota(
        jnp.int32, (LANES, LANES), 1
    )
    vocab_ids = lax.broadcasted_iota(jnp.int32, (LANES, vocab), 1)
    for tile in range(block_len // LANES):
        rows = pl.ds(tile * LANES, LANES)
        logits = inbox[0, rows, :].astype(jnp.float32)
        for part in range(1, parts):
            logits = logits + inbox[part, rows, :].astype(jnp.float32)
        wanted = jnp.where(eye, target_ref[tile : tile + 1, :].astype(jnp.float32), 0.0)
        wanted = jnp.sum(wanted, axis=1, keepdims=True).astype(jnp.int32)
        peak = jnp.max(logits, axis=1, keepdims=True)
        exp_total = jnp.sum(jnp.exp(logits - peak), axis=1, keepdims=True)
        picked = jnp.sum(jnp.where(vocab_ids == wanted, logits, 0.0), axis=1, keepdims=True)
        loss = peak + jnp.log(exp_total) - picked
        loss_ref[tile : tile + 1, :] = jnp.sum(jnp.where(eye, loss, 0.0), axis=0, keepdims=True)
    for copy in copies:
        copy.wait_send()


def local(blocks, parts, streams, short_filter, pole_rates, residues, direct, doc_lengths, targets, unembed):
    block_len, chans = streams.shape[1], streams.shape[2]
    poles, vocab = pole_rates.shape[0], unembed.shape[1]
    groups = chans // GROUP
    f32, bf16 = jnp.float32, jnp.bfloat16
    shape = jax.ShapeDtypeStruct
    vmem = pl.BlockSpec(memory_space=pltpu.VMEM)
    smem = pl.BlockSpec(memory_space=pltpu.SMEM)
    params = functools.partial(pltpu.CompilerParams, vmem_limit_bytes=VMEM_LIMIT)

    def stream_spec(j):
        return pl.BlockSpec((1, block_len, GROUP), lambda g: (j, 0, g))

    rounds = max(1, (blocks - 1).bit_length())
    rows = poles * groups * 8
    filter_spec = pl.BlockSpec((3, 3, GROUP), lambda g: (0, 0, g))
    pole_spec = pl.BlockSpec((poles, GROUP), lambda g: (0, g))
    rows_spec = pl.BlockSpec((rows, LANES), lambda g: (0, 0))
    y_spec = pl.BlockSpec((1, block_len * 8, LANES), lambda g: (g, 0, 0))

    y_local, edges, rates, weights, incoming = pl.pallas_call(
        functools.partial(recur_kernel, blocks, groups),
        name="recur",
        grid=(groups,),
        out_shape=[
            shape((groups, block_len * 8, LANES), f32),
            shape((8, chans), f32),
            shape((rows, LANES), f32),
            shape((rows, LANES), f32),
            shape((rows, LANES), f32),
        ],
        in_specs=[
            smem,
            pl.BlockSpec((3, 16, chans), lambda g: (0, block_len // 16 - 1, 0)),
            stream_spec(1), stream_spec(2), filter_spec, pole_spec, pole_spec,
            pl.BlockSpec((1, GROUP), lambda g: (0, g)),
        ],
        out_specs=[y_spec, pl.BlockSpec((8, chans), lambda g: (0, 0)), rows_spec, rows_spec, rows_spec],
        scratch_shapes=[
            pltpu.VMEM((8 * (block_len + 8), LANES), f32),
            pltpu.VMEM((8 * (block_len + 8), LANES), f32),
            pltpu.VMEM((poles * 8, LANES), f32),
            pltpu.VMEM((block_len * 8, LANES), f32),
            pltpu.VMEM((block_len, LANES), f32),
            pltpu.VMEM((block_len, LANES), f32),
            pltpu.VMEM((2 * poles * 8, LANES), f32),
            pltpu.VMEM((rows, LANES), f32),
            pltpu.VMEM((16, chans // 2), bf16),
            pltpu.VMEM((16, chans // 2), bf16),
            pltpu.VMEM((rounds, rows, LANES), bf16),
            pltpu.VMEM((rounds, rows, LANES), bf16),
            pltpu.SemaphoreType.DMA,
            pltpu.SemaphoreType.DMA,
            pltpu.SemaphoreType.DMA((rounds, groups)),
            pltpu.SemaphoreType.DMA((rounds, groups)),
        ],
        compiler_params=params(collective_id=0, has_side_effects=True),
    )(doc_lengths, streams, streams, streams, short_filter, pole_rates, residues, direct.reshape(1, chans))

    turned_spec = pl.BlockSpec((poles * 8, LANES), lambda g: (g, 0))
    edge_spec = pl.BlockSpec((8, GROUP), lambda g: (0, g))
    gated_out, logits = pl.pallas_call(
        finish_kernel,
        name="finish",
        grid=(groups,),
        out_shape=[shape((block_len, chans), bf16), shape((block_len, vocab), bf16)],
        in_specs=[
            smem, stream_spec(0), edge_spec, filter_spec, turned_spec, turned_spec, turned_spec, y_spec,
            pl.BlockSpec((GROUP, vocab), lambda g: (g, 0)),
        ],
        out_specs=[
            pl.BlockSpec((block_len, GROUP), lambda g: (0, g)),
            pl.BlockSpec((block_len, vocab), lambda g: (0, 0)),
        ],
        scratch_shapes=[
            pltpu.VMEM((8 * (block_len + 8), LANES), f32),
            pltpu.VMEM((block_len * 8, LANES), f32),
            pltpu.VMEM((block_len, vocab), f32),
        ],
        compiler_params=params(),
    )(
        doc_lengths, streams, edges, short_filter, rates, weights,
        incoming, y_local, unembed,
    )

    loss = pl.pallas_call(
        functools.partial(loss_kernel, parts),
        name="loss",
        out_shape=shape((block_len // LANES, LANES), f32),
        in_specs=[vmem, vmem],
        out_specs=vmem,
        scratch_shapes=[
            pltpu.VMEM((parts, block_len, vocab), bf16),
            pltpu.SemaphoreType.DMA((max(1, parts - 1),)),
            pltpu.SemaphoreType.DMA((max(1, parts - 1),)),
        ],
        compiler_params=params(collective_id=1, has_side_effects=True),
    )(logits, targets.reshape(block_len // LANES, LANES))
    return gated_out, loss.reshape(block_len)


def solution(mesh):
    in_specs = (
        P(None, "seq", "chan"),
        P(None, None, "chan"),
        P(None, "chan"),
        P(None, "chan"),
        P("chan"),
        P(),
        P("seq"),
        P("chan", None),
    )
    out_specs = (P("seq", "chan"), P("seq"))
    body = functools.partial(local, mesh.shape["seq"], mesh.shape["chan"])
    return jax.shard_map(body, mesh=mesh, in_specs=in_specs, out_specs=out_specs, check_vma=False)
```

```python
import functools

import jax
import jax.numpy as jnp
from jax import lax
from jax.experimental import pallas as pl
from jax.experimental.pallas import tpu as pltpu
from jax.sharding import PartitionSpec as P

MESH = pl.DeviceIdType.MESH
LANES = 128
GROUP = 8 * LANES
VMEM_LIMIT = 65200 * 1024


def doc_firsts(lengths_ref):
    firsts = [jnp.int32(0)]
    for d in range(lengths_ref.shape[0] - 1):
        firsts.append(firsts[-1] + lengths_ref[d])
    return firsts


def any_between(firsts, low, high):
    found = jnp.bool_(False)
    for first in firsts:
        found = found | ((first >= low) & (first < high))
    return found


def greet(peers):
    barrier = pltpu.get_barrier_semaphore()
    for axis, peer, there in peers:

        @pl.when(there)
        def _():
            pl.semaphore_signal(barrier, inc=1, device_id={axis: peer}, device_id_type=MESH)

    if peers:
        pl.semaphore_wait(barrier, sum(jnp.where(there, 1, 0) for _, _, there in peers))


def load_block(raw, stream_ref):
    block_len = stream_ref.shape[1]

    def step(i, _):
        rows = pl.ds(pl.multiple_of(i * 16, 16), 16)
        for ct in range(8):
            tile = stream_ref[0, rows, pl.ds(ct * LANES, LANES)].astype(jnp.float32)
            raw[pl.ds(pl.multiple_of(i * 128 + ct * 8, 8), 8), :] = tile[0:8]
            raw[pl.ds(pl.multiple_of(i * 128 + 64 + ct * 8, 8), 8), :] = tile[8:16]
        return 0

    lax.fori_loop(0, block_len // 16, step, 0, unroll=2)


def load_taps(filter_ref, turn, stream_id, bank_table, slot):
    for ct in range(8):
        turn[pl.ds(ct * 8, 3), :] = filter_ref[stream_id, :, pl.ds(ct * LANES, LANES)]
    taps = [turn[pl.ds(shift, 8, stride=8), :] for shift in range(3)]
    width = bank_table.shape[0] // 3
    zero = jnp.zeros((8, LANES), jnp.float32)
    for bank, pair in enumerate(((taps[1], taps[2]), (zero, zero), (taps[1], zero))):
        for n in range(2):
            bank_table[pl.ds(bank * width + (slot * 2 + n) * 8, 8), :] = pair[n]
    return taps[0]


def filtered_token(tap, bank_table, bank_row, slot, now, back_1, back_2):
    tap_1 = bank_table[pl.ds(bank_row + slot * 16, 8), :]
    tap_2 = bank_table[pl.ds(bank_row + slot * 16 + 8, 8), :]
    return tap * now + tap_1 * back_1 + tap_2 * back_2


def to_sublanes(ref, scratch, row_count, first_col=0):
    for top in range(0, row_count, 8):
        for ct in range(8):
            scratch[pl.ds(top * 8 + ct * 8, 8), :] = ref[
                top : top + 8, pl.ds(first_col + ct * LANES, LANES)
            ]
    return [scratch[pl.ds((p // 8) * 64 + p % 8, 8, stride=8), :] for p in range(row_count)]


def recur_kernel(
    blocks, groups,
    lengths_ref, tail_ref, k_ref, v_ref, filter_ref, rate_ref, residue_ref, direct_ref,
    y_ref, edge_ref, rate_out, weight_out, in_ref,
    raw_k, raw_v, turn, table, tap_table, ends,
    packed, landed, outbox, inbox, edge_send, edge_recv, send_sem, recv_sem,
):
    block_len = k_ref.shape[1]
    poles = rate_ref.shape[0]
    span = poles * 8
    group = pl.program_id(0)
    me = lax.axis_index("seq")
    first_pos = me * block_len
    firsts = doc_firsts(lengths_ref)
    rounds = max(1, (blocks - 1).bit_length())
    half = packed.shape[1]

    def last_start(pos):
        best = jnp.int32(0)
        for first in firsts:
            best = jnp.maximum(best, jnp.where(first <= pos, first, 0))
        return best

    edge_copy = pltpu.make_async_remote_copy(
        src_ref=packed,
        dst_ref=landed,
        send_sem=edge_send,
        recv_sem=edge_recv,
        device_id={"seq": me + 1},
        device_id_type=MESH,
    )

    def state_copy(k, piece):
        rows = pl.ds(pl.multiple_of(piece * span, span), span)
        return pltpu.make_async_remote_copy(
            src_ref=outbox.at[k, rows],
            dst_ref=inbox.at[k, rows],
            send_sem=send_sem.at[k, piece],
            recv_sem=recv_sem.at[k, piece],
            device_id={"seq": me + (1 << k)},
            device_id_type=MESH,
        )

    own_keep = jnp.where(last_start(first_pos + block_len - 1) < first_pos, 1.0, 0.0)

    def send(k, piece):
        rows = pl.ds(pl.multiple_of(piece * span, span), span)

        @pl.when(me + (1 << k) < blocks)
        def _():
            whole = ends[rows, :]
            if k:
                fade = jnp.exp(-rate_out[rows, :] * float(block_len)) * own_keep
                whole = whole + fade * in_ref[rows, :]
            outbox[k, rows, :] = whole.astype(jnp.bfloat16)
            state_copy(k, piece).start()

    def receive(k, piece):
        rows = pl.ds(pl.multiple_of(piece * span, span), span)
        reach = 1 << k
        far = first_pos - (reach - 1) * block_len

        @pl.when(me >= reach)
        def _():
            state_copy(k, piece).wait_recv()
            got = inbox[k, rows, :].astype(jnp.float32)
            if k:
                clear = jnp.where(last_start(first_pos - 1) < far, 1.0, 0.0)
                got = got * (jnp.exp(-rate_out[rows, :] * float((reach - 1) * block_len)) * clear)
            in_ref[rows, :] += got

    def relay(k, piece):
        receive(k, piece)
        if k + 1 < rounds:
            send(k + 1, piece)

    @pl.when(group == 0)
    def _():
        rows = []
        for side in range(2):
            cols = pl.ds(side * half, half)
            for j in range(3):
                rows.append(tail_ref[j, :, cols].astype(jnp.float32)[14:16])
            rows.append(jnp.zeros((2, half), jnp.float32))
        packed[...] = jnp.concatenate(rows, axis=0).astype(jnp.bfloat16)
        peers = []
        for k in range(rounds):
            peers.append(("seq", me + (1 << k), me + (1 << k) < blocks))
            peers.append(("seq", me - (1 << k), me >= (1 << k)))
        greet(peers)

        @pl.when(me < blocks - 1)
        def _():
            edge_copy.start()

        in_ref[...] = jnp.zeros_like(in_ref)
        table[pl.ds(span, span), :] = jnp.zeros((span, LANES), jnp.float32)

    load_block(raw_k, k_ref)
    load_block(raw_v, v_ref)

    rates = to_sublanes(rate_ref, turn, poles)
    decays = [jnp.exp(-r) for r in rates]
    own = pl.multiple_of(group * span, span)
    for p in range(poles):
        rate_out[pl.ds(own + p * 8, 8), :] = rates[p]
        table[pl.ds(p * 8, 8), :] = decays[p]
    residues = to_sublanes(residue_ref, turn, poles)
    weights = [residues[p] * (1.0 - decays[p]) for p in range(poles)]
    for p in range(poles):
        weight_out[pl.ds(own + p * 8, 8), :] = weights[p]
    for ct in range(8):
        turn[pl.ds(ct * 8, 8), :] = jnp.broadcast_to(direct_ref[:, pl.ds(ct * LANES, LANES)], (8, LANES))
    direct = turn[pl.ds(0, 8, stride=8), :]

    @pl.when(group == 0)
    def _():
        @pl.when(me > 0)
        def _():
            edge_copy.wait_recv()
            got = landed[...].astype(jnp.float32)
            edge_ref[:, pl.ds(0, half)] = got[0:8]
            edge_ref[:, pl.ds(half, half)] = got[8:16]

        @pl.when(me == 0)
        def _():
            edge_ref[...] = jnp.zeros_like(edge_ref)

    edges = to_sublanes(edge_ref, turn, 8, pl.multiple_of(group * GROUP, GROUP))
    k_tap = load_taps(filter_ref, turn, 1, tap_table, 0)
    v_tap = load_taps(filter_ref, turn, 2, tap_table, 1)

    def chunk(i, carry):
        states, (k_1, k_2, v_1, v_2) = list(carry[:poles]), carry[poles:]
        place = first_pos + i * 8
        after = any_between(firsts, place - 1, place)
        for j in range(8):
            rows = pl.ds(i * 64 + j, 8, stride=8)
            starts = any_between(firsts, place + j, place + j + 1)
            bank = jnp.where(starts, span, 0)
            tap_row = jnp.where(starts, 32, jnp.where(after, 64, 0))
            after = starts
            k_0, v_0 = raw_k[rows, :], raw_v[rows, :]
            k = filtered_token(k_tap, tap_table, tap_row, 0, k_0, k_1, k_2)
            v = filtered_token(v_tap, tap_table, tap_row, 1, v_0, v_1, v_2)
            k_1, k_2, v_1, v_2 = k_0, k_1, v_0, v_1
            x = k * v
            sums = [direct * x, None, None, None]
            for p in range(poles):
                states[p] = table[pl.ds(bank + p * 8, 8), :] * states[p] + x
                term = weights[p] * states[p]
                sums[p % 4] = term if sums[p % 4] is None else sums[p % 4] + term
            y_ref[0, rows, :] = (sums[0] + sums[1]) + (sums[2] + sums[3])
        return tuple(states) + (k_1, k_2, v_1, v_2)

    chunks = block_len // 8
    states = tuple(jnp.zeros((8, LANES), jnp.float32) for _ in range(poles))
    states += (edges[3], edges[2], edges[5], edges[4])
    states = lax.fori_loop(0, chunks // 2, chunk, states)
    for k in range(0, rounds, 2):
        piece = group - 1 - k // 2

        @pl.when(piece >= 0)
        def _():
            relay(k, piece)

    states = lax.fori_loop(chunks // 2, chunks, chunk, states)
    for p in range(poles):
        ends[pl.ds(own + p * 8, 8), :] = states[p]
    send(0, group)
    for k in range(1, rounds, 2):
        piece = group - (k + 1) // 2

        @pl.when(piece >= 0)
        def _():
            relay(k, piece)

    @pl.when(group == groups - 1)
    def _():
        for slot in range(2 * groups, 2 * groups + rounds):
            for k in reversed(range(rounds)):
                piece, odd = divmod(slot - 2 - k, 2)
                if odd == 0 and 0 <= piece < groups:
                    relay(k, piece)
        for k in range(rounds):
            for piece in range(groups):

                @pl.when(me + (1 << k) < blocks)
                def _():
                    state_copy(k, piece).wait_send()

        @pl.when(me < blocks - 1)
        def _():
            edge_copy.wait_send()


def finish_kernel(
    lengths_ref, q_ref, edge_ref, filter_ref, rate_ref, weight_ref, in_ref, y_in, unembed_ref,
    gated_ref, logits_ref,
    raw_q, turn, tap_table, gated, total,
):
    block_len = q_ref.shape[1]
    poles = rate_ref.shape[0] // 8
    first_pos = lax.axis_index("seq") * block_len
    firsts = doc_firsts(lengths_ref)
    group = pl.program_id(0)
    cut = jnp.int32(block_len)
    for first in firsts:
        cut = jnp.where(first >= first_pos, jnp.minimum(cut, first - first_pos), cut)
    load_block(raw_q, q_ref)
    edges = to_sublanes(edge_ref, turn, 8)
    q_tap = load_taps(filter_ref, turn, 0, tap_table, 0)
    tiles = [pl.ds(p * 8, 8) for p in range(poles)]
    decays = [jnp.exp(-rate_ref[tile, :]) for tile in tiles]
    fading = tuple(weight_ref[tile, :] * in_ref[tile, :] * d for tile, d in zip(tiles, decays))

    def gate_chunk(i, carry, carried):
        (q_1, q_2), fading = carry[:2], carry[2:]
        place = first_pos + i * 8
        after = any_between(firsts, place - 1, place)
        for j in range(8):
            rows = pl.ds(i * 64 + j, 8, stride=8)
            starts = any_between(firsts, place + j, place + j + 1)
            tap_row = jnp.where(starts, 16, jnp.where(after, 32, 0))
            after = starts
            q_0 = raw_q[rows, :]
            q = filtered_token(q_tap, tap_table, tap_row, 0, q_0, q_1, q_2)
            q_1, q_2 = q_0, q_1
            y = y_in[0, rows, :]
            if carried:
                sums = list(fading[:4])
                for p in range(4, poles):
                    sums[p % 4] = sums[p % 4] + fading[p]
                arrived = (sums[0] + sums[1]) + (sums[2] + sums[3])
                y = y + jnp.where(i * 8 + j < cut, 1.0, 0.0) * arrived
                fading = [f * d for f, d in zip(fading, decays)]
            gated[rows, :] = q * y
        return (q_1, q_2) + tuple(fading)

    carried = (cut + 7) // 8
    carry = (edges[1], edges[0]) + fading
    carry = lax.fori_loop(0, carried, functools.partial(gate_chunk, carried=True), carry)
    lax.fori_loop(carried, block_len // 8, functools.partial(gate_chunk, carried=False), carry[:2])

    def round_step(i, _):
        for ct in range(8):
            halves = [
                gated[pl.ds(pl.multiple_of(i * 128 + side * 64 + ct * 8, 8), 8), :] for side in range(2)
            ]
            both = jnp.concatenate(halves, axis=0).astype(jnp.bfloat16)
            gated_ref[pl.ds(pl.multiple_of(i * 16, 16), 16), pl.ds(ct * LANES, LANES)] = both
        return 0

    lax.fori_loop(0, block_len // 16, round_step, 0, unroll=2)
    part = jnp.dot(gated_ref[...], unembed_ref[...], preferred_element_type=jnp.float32)

    @pl.when(group == 0)
    def _():
        total[...] = part

    @pl.when(group > 0)
    def _():
        total[...] += part

    @pl.when(group == pl.num_programs(0) - 1)
    def _():
        logits_ref[...] = total[...].astype(jnp.bfloat16)


def loss_kernel(parts, logits_ref, target_ref, loss_ref, inbox, send_sem, recv_sem):
    me = lax.axis_index("chan")
    others = [lax.rem(me + d, parts) for d in range(1, parts)]
    greet([("chan", other, me >= 0) for other in others])
    copies = []
    for d in range(1, parts):
        copies.append(
            pltpu.make_async_remote_copy(
                src_ref=logits_ref,
                dst_ref=inbox.at[me],
                send_sem=send_sem.at[d - 1],
                recv_sem=recv_sem.at[d - 1],
                device_id={"chan": others[d - 1]},
                device_id_type=MESH,
            )
        )
        copies[-1].start()
    inbox[me] = logits_ref[...]
    for copy in copies:
        copy.wait_recv()
    block_len, vocab = logits_ref.shape
    eye = lax.broadcasted_iota(jnp.int32, (LANES, LANES), 0) == lax.broadcasted_iota(
        jnp.int32, (LANES, LANES), 1
    )
    vocab_ids = lax.broadcasted_iota(jnp.int32, (LANES, vocab), 1)
    for tile in range(block_len // LANES):
        rows = pl.ds(tile * LANES, LANES)
        logits = inbox[0, rows, :].astype(jnp.float32)
        for part in range(1, parts):
            logits = logits + inbox[part, rows, :].astype(jnp.float32)
        wanted = jnp.where(eye, target_ref[tile : tile + 1, :].astype(jnp.float32), 0.0)
        wanted = jnp.sum(wanted, axis=1, keepdims=True).astype(jnp.int32)
        peak = jnp.max(logits, axis=1, keepdims=True)
        exp_total = jnp.sum(jnp.exp(logits - peak), axis=1, keepdims=True)
        picked = jnp.sum(jnp.where(vocab_ids == wanted, logits, 0.0), axis=1, keepdims=True)
        loss = peak + jnp.log(exp_total) - picked
        loss_ref[tile : tile + 1, :] = jnp.sum(jnp.where(eye, loss, 0.0), axis=0, keepdims=True)
    for copy in copies:
        copy.wait_send()


def local(blocks, parts, streams, short_filter, pole_rates, residues, direct, doc_lengths, targets, unembed):
    block_len, chans = streams.shape[1], streams.shape[2]
    poles, vocab = pole_rates.shape[0], unembed.shape[1]
    groups = chans // GROUP
    f32, bf16 = jnp.float32, jnp.bfloat16
    shape = jax.ShapeDtypeStruct
    vmem = pl.BlockSpec(memory_space=pltpu.VMEM)
    smem = pl.BlockSpec(memory_space=pltpu.SMEM)
    params = functools.partial(pltpu.CompilerParams, vmem_limit_bytes=VMEM_LIMIT)

    def stream_spec(j):
        return pl.BlockSpec((1, block_len, GROUP), lambda g: (j, 0, g))

    rounds = max(1, (blocks - 1).bit_length())
    rows = poles * groups * 8
    filter_spec = pl.BlockSpec((3, 3, GROUP), lambda g: (0, 0, g))
    pole_spec = pl.BlockSpec((poles, GROUP), lambda g: (0, g))
    rows_spec = pl.BlockSpec((rows, LANES), lambda g: (0, 0))
    y_spec = pl.BlockSpec((1, block_len * 8, LANES), lambda g: (g, 0, 0))

    y_local, edges, rates, weights, incoming = pl.pallas_call(
        functools.partial(recur_kernel, blocks, groups),
        name="recur",
        grid=(groups,),
        out_shape=[
            shape((groups, block_len * 8, LANES), f32),
            shape((8, chans), f32),
            shape((rows, LANES), f32),
            shape((rows, LANES), f32),
            shape((rows, LANES), f32),
        ],
        in_specs=[
            smem,
            pl.BlockSpec((3, 16, chans), lambda g: (0, block_len // 16 - 1, 0)),
            stream_spec(1), stream_spec(2), filter_spec, pole_spec, pole_spec,
            pl.BlockSpec((1, GROUP), lambda g: (0, g)),
        ],
        out_specs=[y_spec, pl.BlockSpec((8, chans), lambda g: (0, 0)), rows_spec, rows_spec, rows_spec],
        scratch_shapes=[
            pltpu.VMEM((block_len * 8, LANES), f32),
            pltpu.VMEM((block_len * 8, LANES), f32),
            pltpu.VMEM((poles * 8, LANES), f32),
            pltpu.VMEM((2 * poles * 8, LANES), f32),
            pltpu.VMEM((96, LANES), f32),
            pltpu.VMEM((rows, LANES), f32),
            pltpu.VMEM((16, chans // 2), bf16),
            pltpu.VMEM((16, chans // 2), bf16),
            pltpu.VMEM((rounds, rows, LANES), bf16),
            pltpu.VMEM((rounds, rows, LANES), bf16),
            pltpu.SemaphoreType.DMA,
            pltpu.SemaphoreType.DMA,
            pltpu.SemaphoreType.DMA((rounds, groups)),
            pltpu.SemaphoreType.DMA((rounds, groups)),
        ],
        compiler_params=params(collective_id=0, has_side_effects=True),
    )(doc_lengths, streams, streams, streams, short_filter, pole_rates, residues, direct.reshape(1, chans))

    turned_spec = pl.BlockSpec((poles * 8, LANES), lambda g: (g, 0))
    edge_spec = pl.BlockSpec((8, GROUP), lambda g: (0, g))
    gated_out, logits = pl.pallas_call(
        finish_kernel,
        name="finish",
        grid=(groups,),
        out_shape=[shape((block_len, chans), bf16), shape((block_len, vocab), bf16)],
        in_specs=[
            smem, stream_spec(0), edge_spec, filter_spec, turned_spec, turned_spec, turned_spec, y_spec,
            pl.BlockSpec((GROUP, vocab), lambda g: (g, 0)),
        ],
        out_specs=[
            pl.BlockSpec((block_len, GROUP), lambda g: (0, g)),
            pl.BlockSpec((block_len, vocab), lambda g: (0, 0)),
        ],
        scratch_shapes=[
            pltpu.VMEM((block_len * 8, LANES), f32),
            pltpu.VMEM((64, LANES), f32),
            pltpu.VMEM((48, LANES), f32),
            pltpu.VMEM((block_len * 8, LANES), f32),
            pltpu.VMEM((block_len, vocab), f32),
        ],
        compiler_params=params(),
    )(
        doc_lengths, streams, edges, short_filter, rates, weights,
        incoming, y_local, unembed,
    )

    loss = pl.pallas_call(
        functools.partial(loss_kernel, parts),
        name="loss",
        out_shape=shape((block_len // LANES, LANES), f32),
        in_specs=[vmem, vmem],
        out_specs=vmem,
        scratch_shapes=[
            pltpu.VMEM((parts, block_len, vocab), bf16),
            pltpu.SemaphoreType.DMA((max(1, parts - 1),)),
            pltpu.SemaphoreType.DMA((max(1, parts - 1),)),
        ],
        compiler_params=params(collective_id=1, has_side_effects=True),
    )(logits, targets.reshape(block_len // LANES, LANES))
    return gated_out, loss.reshape(block_len)


def solution(mesh):
    in_specs = (
        P(None, "seq", "chan"),
        P(None, None, "chan"),
        P(None, "chan"),
        P(None, "chan"),
        P("chan"),
        P(),
        P("seq"),
        P("chan", None),
    )
    out_specs = (P("seq", "chan"), P("seq"))
    body = functools.partial(local, mesh.shape["seq"], mesh.shape["chan"])
    return jax.shard_map(body, mesh=mesh, in_specs=in_specs, out_specs=out_specs, check_vma=False)
```

```python
import functools

import jax
import jax.numpy as jnp
from jax import lax
from jax.experimental import pallas as pl
from jax.experimental.pallas import tpu as pltpu
from jax.sharding import PartitionSpec as P

MESH = pl.DeviceIdType.MESH
LANES = 128
GROUP = 8 * LANES
VMEM_LIMIT = 40 * 1024 * 1024
RECUR_VMEM_LIMIT = 56 * 1024 * 1024


def doc_firsts(lengths_ref):
    firsts = [jnp.int32(0)]
    for d in range(lengths_ref.shape[0] - 1):
        firsts.append(firsts[-1] + lengths_ref[d])
    return firsts


def any_between(firsts, low, high):
    found = jnp.bool_(False)
    for first in firsts:
        found = found | ((first >= low) & (first < high))
    return found


def greet(peers):
    barrier = pltpu.get_barrier_semaphore()
    for axis, peer, there in peers:

        @pl.when(there)
        def _():
            pl.semaphore_signal(barrier, inc=1, device_id={axis: peer}, device_id_type=MESH)

    if peers:
        pl.semaphore_wait(barrier, sum(jnp.where(there, 1, 0) for _, _, there in peers))


def load_edge(ext, edge_ref, stream_id, first_col=0):
    pitch = ext.shape[0] // 8
    for ct in range(8):
        edge = edge_ref[:, pl.ds(first_col + ct * LANES, LANES)]
        both = jnp.concatenate([edge[0:6], edge[2 * stream_id : 2 * stream_id + 2]], axis=0)
        ext[pl.ds(ct * pitch, 8), :] = both


def load_block(ext, stream_ref):
    block_len = stream_ref.shape[1]
    pitch = block_len + 8

    def step(i, _):
        rows = pl.ds(pl.multiple_of(i * 16, 16), 16)
        for ct in range(8):
            tile = stream_ref[0, rows, pl.ds(ct * LANES, LANES)].astype(jnp.float32)
            ext[pl.ds(pl.multiple_of(ct * pitch + i * 16 + 8, 8), 16), :] = tile
        return 0

    lax.fori_loop(0, block_len // 16, step, 0)


def load_taps(filter_ref, stream_id, ct):
    cols = pl.ds(ct * LANES, LANES)
    return [
        jnp.broadcast_to(filter_ref[stream_id, shift : shift + 1, cols], (8, LANES)) for shift in range(3)
    ]


def filter_tile(ext, taps, i, ct, masks=None):
    pitch = ext.shape[0] // 8
    terms = []
    for shift in range(3):
        term = taps[shift] * ext[pl.ds(ct * pitch + i * 8 + (8 - shift), 8), :]
        if shift and masks is not None:
            term = term * masks[shift - 1]
        terms.append(term)
    return terms[0] + terms[1] + terms[2]


def at_starts(firsts, first_pos, block_len, tile_len, redo):
    for first in firsts:
        for after in range(2):
            place = first + after - first_pos

            @pl.when((place >= 0) & (place < block_len))
            def _():
                redo(place // tile_len)


def tile_masks(firsts, base):
    pos = base + lax.broadcasted_iota(jnp.int32, (8, LANES), 0)
    start = jnp.zeros((8, LANES), jnp.int32)
    for first in firsts:
        start = jnp.maximum(start, jnp.where(first <= pos, first, 0))
    return [pos - shift >= start for shift in (1, 2)]


def load_tiles(raw, stream_ref):
    block_len = stream_ref.shape[1]

    def step(i, _):
        rows = pl.ds(pl.multiple_of(i * 16, 16), 16)
        for ct in range(8):
            tile = stream_ref[0, rows, pl.ds(ct * LANES, LANES)].astype(jnp.float32)
            raw[pl.ds(pl.multiple_of(i * 128 + ct * 8, 8), 8), :] = tile[0:8]
            raw[pl.ds(pl.multiple_of(i * 128 + 64 + ct * 8, 8), 8), :] = tile[8:16]
        return 0

    lax.fori_loop(0, block_len // 16, step, 0, unroll=2)


def turned_taps(filter_ref, turn, stream_id, first_col):
    for ct in range(8):
        turn[pl.ds(ct * 8, 3), :] = filter_ref[stream_id, :, pl.ds(first_col + ct * LANES, LANES)]
    return [turn[pl.ds(shift, 8, stride=8), :] for shift in range(3)]


def to_sublanes(ref, scratch, row_count, first_col=0):
    for top in range(0, row_count, 8):
        for ct in range(8):
            scratch[pl.ds(top * 8 + ct * 8, 8), :] = ref[
                top : top + 8, pl.ds(first_col + ct * LANES, LANES)
            ]
    return [scratch[pl.ds((p // 8) * 64 + p % 8, 8, stride=8), :] for p in range(row_count)]


def recur_kernel(
    blocks, groups,
    lengths_ref, tail_ref, k_ref, v_ref, filter_hbm, rate_hbm, residue_hbm, direct_hbm,
    y_ref, edge_ref, rate_out, weight_out, in_ref,
    raw_k, raw_v, turn, keeps, ends, filter_ref, rate_ref, residue_ref, direct_ref, fetch_sem,
    packed, landed, outbox, inbox, edge_send, edge_recv, send_sem, recv_sem,
):
    block_len = k_ref.shape[1]
    poles = rate_ref.shape[0]
    span = poles * 8
    group = pl.program_id(0)
    me = lax.axis_index("seq")
    first_pos = me * block_len
    firsts = doc_firsts(lengths_ref)
    rounds = max(1, (blocks - 1).bit_length())
    half = packed.shape[1]

    def last_start(pos):
        best = jnp.int32(0)
        for first in firsts:
            best = jnp.maximum(best, jnp.where(first <= pos, first, 0))
        return best

    edge_copy = pltpu.make_async_remote_copy(
        src_ref=packed,
        dst_ref=landed,
        send_sem=edge_send,
        recv_sem=edge_recv,
        device_id={"seq": me + 1},
        device_id_type=MESH,
    )

    def state_copy(k, piece):
        rows = pl.ds(pl.multiple_of(piece * span, span), span)
        return pltpu.make_async_remote_copy(
            src_ref=outbox.at[k, rows],
            dst_ref=inbox.at[k, rows],
            send_sem=send_sem.at[k, piece],
            recv_sem=recv_sem.at[k, piece],
            device_id={"seq": me + (1 << k)},
            device_id_type=MESH,
        )

    own_keep = jnp.where(last_start(first_pos + block_len - 1) < first_pos, 1.0, 0.0)

    def send(k, piece):
        rows = pl.ds(pl.multiple_of(piece * span, span), span)

        @pl.when(me + (1 << k) < blocks)
        def _():
            whole = ends[rows, :]
            if k:
                fade = jnp.exp(-rate_out[rows, :] * float(block_len)) * own_keep
                whole = whole + fade * in_ref[rows, :]
            outbox[k, rows, :] = whole.astype(jnp.bfloat16)
            state_copy(k, piece).start()

    def receive(k, piece):
        rows = pl.ds(pl.multiple_of(piece * span, span), span)
        reach = 1 << k
        far = first_pos - (reach - 1) * block_len

        @pl.when(me >= reach)
        def _():
            state_copy(k, piece).wait_recv()
            got = inbox[k, rows, :].astype(jnp.float32)
            if k:
                clear = jnp.where(last_start(first_pos - 1) < far, 1.0, 0.0)
                got = got * (jnp.exp(-rate_out[rows, :] * float((reach - 1) * block_len)) * clear)
            in_ref[rows, :] += got

    def relay(k, piece):
        receive(k, piece)
        if k + 1 < rounds:
            send(k + 1, piece)

    fetches = [
        pltpu.make_async_copy(src, dst, fetch_sem.at[n])
        for n, (src, dst) in enumerate(
            (
                (filter_hbm, filter_ref),
                (rate_hbm, rate_ref),
                (residue_hbm, residue_ref),
                (direct_hbm, direct_ref),
            )
        )
    ]

    @pl.when(group == 0)
    def _():
        for fetch in fetches:
            fetch.start()
        rows = []
        for side in range(2):
            cols = pl.ds(side * half, half)
            for j in range(3):
                rows.append(tail_ref[j, :, cols].astype(jnp.float32)[14:16])
            rows.append(jnp.zeros((2, half), jnp.float32))
        packed[...] = jnp.concatenate(rows, axis=0).astype(jnp.bfloat16)
        peers = []
        for k in range(rounds):
            peers.append(("seq", me + (1 << k), me + (1 << k) < blocks))
            peers.append(("seq", me - (1 << k), me >= (1 << k)))
        greet(peers)

        @pl.when(me < blocks - 1)
        def _():
            edge_copy.start()

        in_ref[...] = jnp.zeros_like(in_ref)

        def keep_step(i, _):
            place = first_pos + i * 8 + lax.broadcasted_iota(jnp.int32, (64, LANES), 0) // 8
            keep = jnp.ones((64, LANES), jnp.float32)
            for first in firsts:
                keep = jnp.where(place == first, 0.0, keep)
            keeps[pl.ds(pl.multiple_of(i * 64, 64), 64), :] = keep
            return 0

        lax.fori_loop(0, block_len // 8, keep_step, 0)
        for fetch in fetches:
            fetch.wait()

    load_tiles(raw_k, k_ref)
    load_tiles(raw_v, v_ref)
    first_col = pl.multiple_of(group * GROUP, GROUP)

    rates = to_sublanes(rate_ref, turn, poles, first_col)
    decays = [jnp.exp(-r) for r in rates]
    own = pl.multiple_of(group * span, span)
    for p in range(poles):
        rate_out[pl.ds(own + p * 8, 8), :] = rates[p]
    residues = to_sublanes(residue_ref, turn, poles, first_col)
    weights = [residues[p] * (1.0 - decays[p]) for p in range(poles)]
    for p in range(poles):
        weight_out[pl.ds(own + p * 8, 8), :] = weights[p]
    for ct in range(8):
        turn[pl.ds(ct * 8, 8), :] = jnp.broadcast_to(
            direct_ref[:, pl.ds(first_col + ct * LANES, LANES)], (8, LANES)
        )
    direct = turn[pl.ds(0, 8, stride=8), :]

    @pl.when(group == 0)
    def _():
        @pl.when(me > 0)
        def _():
            edge_copy.wait_recv()
            got = landed[...].astype(jnp.float32)
            edge_ref[:, pl.ds(0, half)] = got[0:8]
            edge_ref[:, pl.ds(half, half)] = got[8:16]

        @pl.when(me == 0)
        def _():
            edge_ref[...] = jnp.zeros_like(edge_ref)

    edges = to_sublanes(edge_ref, turn, 8, first_col)
    k_taps = turned_taps(filter_ref, turn, 1, first_col)
    v_taps = turned_taps(filter_ref, turn, 2, first_col)

    def chunk(i, carry):
        states, (k_1, k_2, v_1, v_2) = list(carry[:poles]), carry[poles:]
        for j in range(8):
            rows = pl.ds(i * 64 + j, 8, stride=8)
            keep = keeps[pl.ds(pl.multiple_of(i * 64 + j * 8, 8), 8), :]
            k_0, v_0 = raw_k[rows, :], raw_v[rows, :]
            k_1, k_2, v_1, v_2 = k_1 * keep, k_2 * keep, v_1 * keep, v_2 * keep
            k = k_taps[0] * k_0 + k_taps[1] * k_1 + k_taps[2] * k_2
            v = v_taps[0] * v_0 + v_taps[1] * v_1 + v_taps[2] * v_2
            k_1, k_2, v_1, v_2 = k_0, k_1, v_0, v_1
            x = k * v
            sums = [direct * x, None, None, None]
            for p in range(poles):
                states[p] = (decays[p] * keep) * states[p] + x
                term = weights[p] * states[p]
                sums[p % 4] = term if sums[p % 4] is None else sums[p % 4] + term
            y_ref[0, rows, :] = (sums[0] + sums[1]) + (sums[2] + sums[3])
        return tuple(states) + (k_1, k_2, v_1, v_2)

    chunks = block_len // 8
    states = tuple(jnp.zeros((8, LANES), jnp.float32) for _ in range(poles))
    states += (edges[3], edges[2], edges[5], edges[4])
    states = lax.fori_loop(0, chunks // 2, chunk, states)
    for k in range(0, rounds, 2):
        piece = group - 1 - k // 2

        @pl.when(piece >= 0)
        def _():
            relay(k, piece)

    states = lax.fori_loop(chunks // 2, chunks, chunk, states)
    for p in range(poles):
        ends[pl.ds(own + p * 8, 8), :] = states[p]
    send(0, group)
    for k in range(1, rounds, 2):
        piece = group - (k + 1) // 2

        @pl.when(piece >= 0)
        def _():
            relay(k, piece)

    @pl.when(group == groups - 1)
    def _():
        for slot in range(2 * groups, 2 * groups + rounds):
            for k in reversed(range(rounds)):
                piece, odd = divmod(slot - 2 - k, 2)
                if odd == 0 and 0 <= piece < groups:
                    relay(k, piece)
        for k in range(rounds):
            for piece in range(groups):

                @pl.when(me + (1 << k) < blocks)
                def _():
                    state_copy(k, piece).wait_send()

        @pl.when(me < blocks - 1)
        def _():
            edge_copy.wait_send()


def finish_kernel(
    lengths_ref, q_ref, edge_ref, filter_ref, rate_ref, weight_ref, in_ref, y_in, unembed_ref,
    gated_ref, logits_ref,
    ext_q, y, total,
):
    block_len = q_ref.shape[1]
    poles = rate_ref.shape[0] // 8
    first_pos = lax.axis_index("seq") * block_len
    firsts = doc_firsts(lengths_ref)
    group = pl.program_id(0)
    cut = jnp.int32(block_len)
    for first in firsts:
        cut = jnp.where(first >= first_pos, jnp.minimum(cut, first - first_pos), cut)
    load_block(ext_q, q_ref)
    load_edge(ext_q, edge_ref, 0)
    tiles = [pl.ds(p * 8, 8) for p in range(poles)]
    decays = [jnp.exp(-rate_ref[tile, :]) for tile in tiles]
    fading = tuple(weight_ref[tile, :] * in_ref[tile, :] * d for tile, d in zip(tiles, decays))

    def fade_chunk(i, fading):
        fading = list(fading)
        for j in range(8):
            sums = [fading[0], fading[1], fading[2], fading[3]]
            for p in range(4, poles):
                sums[p % 4] = sums[p % 4] + fading[p]
            arrived = (sums[0] + sums[1]) + (sums[2] + sums[3])
            rows = pl.ds(i * 64 + j, 8, stride=8)
            y[rows, :] = jnp.where(i * 8 + j < cut, 1.0, 0.0) * arrived
            fading = [f * d for f, d in zip(fading, decays)]
        return tuple(fading)

    carried = (cut + 7) // 8
    lax.fori_loop(0, carried, fade_chunk, fading)

    def plain_chunk(i, _):
        rows = pl.ds(pl.multiple_of(i * 64, 64), 64)
        y[rows, :] = jnp.zeros((64, LANES), jnp.float32)
        return 0

    lax.fori_loop(carried, block_len // 8, plain_chunk, 0)

    def gate(i, ct, taps, masks):
        halves = []
        for side in range(2):
            tile = i * 2 + side
            q = filter_tile(ext_q, taps, tile, ct, masks[side])
            rows = pl.ds(pl.multiple_of(tile * 64 + ct * 8, 8), 8)
            halves.append(q * (y_in[0, rows, :] + y[rows, :]))
        both = jnp.concatenate(halves, axis=0).astype(jnp.bfloat16)
        gated_ref[pl.ds(pl.multiple_of(i * 16, 16), 16), pl.ds(ct * LANES, LANES)] = both

    for ct in range(8):
        taps = load_taps(filter_ref, 0, ct)

        def gate_step(i, _):
            gate(i, ct, taps, [None, None])
            return 0

        lax.fori_loop(0, block_len // 16, gate_step, 0, unroll=4)

    def regate(i):
        masks = []
        for side in range(2):
            pair = tile_masks(firsts, first_pos + i * 16 + side * 8)
            masks.append([jnp.where(m, 1.0, 0.0) for m in pair])
        for ct in range(8):
            gate(i, ct, load_taps(filter_ref, 0, ct), masks)

    at_starts(firsts, first_pos, block_len, 16, regate)
    part = jnp.dot(gated_ref[...], unembed_ref[...], preferred_element_type=jnp.float32)

    @pl.when(group == 0)
    def _():
        total[...] = part

    @pl.when(group > 0)
    def _():
        total[...] += part

    @pl.when(group == pl.num_programs(0) - 1)
    def _():
        logits_ref[...] = total[...].astype(jnp.bfloat16)


def loss_kernel(parts, logits_ref, target_ref, loss_ref, inbox, send_sem, recv_sem):
    me = lax.axis_index("chan")
    others = [lax.rem(me + d, parts) for d in range(1, parts)]
    greet([("chan", other, me >= 0) for other in others])
    copies = []
    for d in range(1, parts):
        copies.append(
            pltpu.make_async_remote_copy(
                src_ref=logits_ref,
                dst_ref=inbox.at[me],
                send_sem=send_sem.at[d - 1],
                recv_sem=recv_sem.at[d - 1],
                device_id={"chan": others[d - 1]},
                device_id_type=MESH,
            )
        )
        copies[-1].start()
    inbox[me] = logits_ref[...]
    for copy in copies:
        copy.wait_recv()
    block_len, vocab = logits_ref.shape
    eye = lax.broadcasted_iota(jnp.int32, (LANES, LANES), 0) == lax.broadcasted_iota(
        jnp.int32, (LANES, LANES), 1
    )
    vocab_ids = lax.broadcasted_iota(jnp.int32, (LANES, vocab), 1)
    for tile in range(block_len // LANES):
        rows = pl.ds(tile * LANES, LANES)
        logits = inbox[0, rows, :].astype(jnp.float32)
        for part in range(1, parts):
            logits = logits + inbox[part, rows, :].astype(jnp.float32)
        wanted = jnp.where(eye, target_ref[tile : tile + 1, :].astype(jnp.float32), 0.0)
        wanted = jnp.sum(wanted, axis=1, keepdims=True).astype(jnp.int32)
        peak = jnp.max(logits, axis=1, keepdims=True)
        exp_total = jnp.sum(jnp.exp(logits - peak), axis=1, keepdims=True)
        picked = jnp.sum(jnp.where(vocab_ids == wanted, logits, 0.0), axis=1, keepdims=True)
        loss = peak + jnp.log(exp_total) - picked
        loss_ref[tile : tile + 1, :] = jnp.sum(jnp.where(eye, loss, 0.0), axis=0, keepdims=True)
    for copy in copies:
        copy.wait_send()


def local(blocks, parts, streams, short_filter, pole_rates, residues, direct, doc_lengths, targets, unembed):
    block_len, chans = streams.shape[1], streams.shape[2]
    poles, vocab = pole_rates.shape[0], unembed.shape[1]
    groups = chans // GROUP
    f32, bf16 = jnp.float32, jnp.bfloat16
    shape = jax.ShapeDtypeStruct
    vmem = pl.BlockSpec(memory_space=pltpu.VMEM)
    hbm = pl.BlockSpec(memory_space=pltpu.HBM)
    smem = pl.BlockSpec(memory_space=pltpu.SMEM)
    params = functools.partial(pltpu.CompilerParams, has_side_effects=True)

    def stream_spec(j):
        return pl.BlockSpec((1, block_len, GROUP), lambda g: (j, 0, g))

    rounds = max(1, (blocks - 1).bit_length())
    rows = poles * groups * 8
    filter_spec = pl.BlockSpec((3, 3, GROUP), lambda g: (0, 0, g))
    rows_spec = pl.BlockSpec((rows, LANES), lambda g: (0, 0))
    y_spec = pl.BlockSpec((1, block_len * 8, LANES), lambda g: (g, 0, 0))

    y_local, edges, rates, weights, incoming = pl.pallas_call(
        functools.partial(recur_kernel, blocks, groups),
        name="recur",
        grid=(groups,),
        out_shape=[
            shape((groups, block_len * 8, LANES), f32),
            shape((8, chans), f32),
            shape((rows, LANES), f32),
            shape((rows, LANES), f32),
            shape((rows, LANES), f32),
        ],
        in_specs=[
            smem,
            pl.BlockSpec((3, 16, chans), lambda g: (0, block_len // 16 - 1, 0)),
            stream_spec(1), stream_spec(2), hbm, hbm, hbm, hbm,
        ],
        out_specs=[y_spec, pl.BlockSpec((8, chans), lambda g: (0, 0)), rows_spec, rows_spec, rows_spec],
        scratch_shapes=[
            pltpu.VMEM((block_len * 8, LANES), f32),
            pltpu.VMEM((block_len * 8, LANES), f32),
            pltpu.VMEM((poles * 8, LANES), f32),
            pltpu.VMEM((block_len * 8, LANES), f32),
            pltpu.VMEM((rows, LANES), f32),
            pltpu.VMEM((3, 3, chans), f32),
            pltpu.VMEM((poles, chans), f32),
            pltpu.VMEM((poles, chans), f32),
            pltpu.VMEM((1, chans), f32),
            pltpu.SemaphoreType.DMA((4,)),
            pltpu.VMEM((16, chans // 2), bf16),
            pltpu.VMEM((16, chans // 2), bf16),
            pltpu.VMEM((rounds, rows, LANES), bf16),
            pltpu.VMEM((rounds, rows, LANES), bf16),
            pltpu.SemaphoreType.DMA,
            pltpu.SemaphoreType.DMA,
            pltpu.SemaphoreType.DMA((rounds, groups)),
            pltpu.SemaphoreType.DMA((rounds, groups)),
        ],
        compiler_params=params(collective_id=0, vmem_limit_bytes=RECUR_VMEM_LIMIT),
    )(doc_lengths, streams, streams, streams, short_filter, pole_rates, residues, direct.reshape(1, chans))

    turned_spec = pl.BlockSpec((poles * 8, LANES), lambda g: (g, 0))
    edge_spec = pl.BlockSpec((8, GROUP), lambda g: (0, g))
    gated_out, logits = pl.pallas_call(
        finish_kernel,
        name="finish",
        grid=(groups,),
        out_shape=[shape((block_len, chans), bf16), shape((block_len, vocab), bf16)],
        in_specs=[
            smem, stream_spec(0), edge_spec, filter_spec, turned_spec, turned_spec, turned_spec, y_spec,
            pl.BlockSpec((GROUP, vocab), lambda g: (g, 0)),
        ],
        out_specs=[
            pl.BlockSpec((block_len, GROUP), lambda g: (0, g)),
            pl.BlockSpec((block_len, vocab), lambda g: (0, 0)),
        ],
        scratch_shapes=[
            pltpu.VMEM((8 * (block_len + 8), LANES), f32),
            pltpu.VMEM((block_len * 8, LANES), f32),
            pltpu.VMEM((block_len, vocab), f32),
        ],
        compiler_params=pltpu.CompilerParams(vmem_limit_bytes=VMEM_LIMIT),
    )(
        doc_lengths, streams, edges, short_filter, rates, weights,
        incoming, y_local, unembed,
    )

    loss = pl.pallas_call(
        functools.partial(loss_kernel, parts),
        name="loss",
        out_shape=shape((block_len // LANES, LANES), f32),
        in_specs=[vmem, vmem],
        out_specs=vmem,
        scratch_shapes=[
            pltpu.VMEM((parts, block_len, vocab), bf16),
            pltpu.SemaphoreType.DMA((max(1, parts - 1),)),
            pltpu.SemaphoreType.DMA((max(1, parts - 1),)),
        ],
        compiler_params=params(collective_id=1, vmem_limit_bytes=VMEM_LIMIT),
    )(logits, targets.reshape(block_len // LANES, LANES))
    return gated_out, loss.reshape(block_len)


def solution(mesh):
    in_specs = (
        P(None, "seq", "chan"),
        P(None, None, "chan"),
        P(None, "chan"),
        P(None, "chan"),
        P("chan"),
        P(),
        P("seq"),
        P("chan", None),
    )
    out_specs = (P("seq", "chan"), P("seq"))
    body = functools.partial(local, mesh.shape["seq"], mesh.shape["chan"])
    return jax.shard_map(body, mesh=mesh, in_specs=in_specs, out_specs=out_specs, check_vma=False)
```

```python
import functools

import jax
import jax.numpy as jnp
from jax import lax
from jax.experimental import pallas as pl
from jax.experimental.pallas import tpu as pltpu
from jax.sharding import PartitionSpec as P

MESH = pl.DeviceIdType.MESH
LANES = 128
GROUP = 8 * LANES
VMEM_LIMIT = 65200 * 1024
LOSS_VMEM_LIMIT = 40 * 1024 * 1024


def doc_firsts(lengths_ref):
    firsts = [jnp.int32(0)]
    for d in range(lengths_ref.shape[0] - 1):
        firsts.append(firsts[-1] + lengths_ref[d])
    return firsts


def any_between(firsts, low, high):
    found = jnp.bool_(False)
    for first in firsts:
        found = found | ((first >= low) & (first < high))
    return found


def greet(peers):
    barrier = pltpu.get_barrier_semaphore()
    for axis, peer, there in peers:

        @pl.when(there)
        def _():
            pl.semaphore_signal(barrier, inc=1, device_id={axis: peer}, device_id_type=MESH)

    if peers:
        pl.semaphore_wait(barrier, sum(jnp.where(there, 1, 0) for _, _, there in peers))


def load_edge(ext, edge_ref, stream_id, first_col=0):
    pitch = ext.shape[0] // 8
    for ct in range(8):
        edge = edge_ref[:, pl.ds(first_col + ct * LANES, LANES)]
        both = jnp.concatenate([edge[0:6], edge[2 * stream_id : 2 * stream_id + 2]], axis=0)
        ext[pl.ds(ct * pitch, 8), :] = both


def load_block(ext, stream_ref):
    block_len = stream_ref.shape[1]
    pitch = block_len + 8

    def step(i, _):
        rows = pl.ds(pl.multiple_of(i * 16, 16), 16)
        for ct in range(8):
            tile = stream_ref[0, rows, pl.ds(ct * LANES, LANES)].astype(jnp.float32)
            ext[pl.ds(pl.multiple_of(ct * pitch + i * 16 + 8, 8), 16), :] = tile
        return 0

    lax.fori_loop(0, block_len // 16, step, 0)


def load_taps(filter_ref, stream_id, ct):
    cols = pl.ds(ct * LANES, LANES)
    return [
        jnp.broadcast_to(filter_ref[stream_id, shift : shift + 1, cols], (8, LANES)) for shift in range(3)
    ]


def filter_tile(ext, taps, i, ct, masks=None):
    pitch = ext.shape[0] // 8
    terms = []
    for shift in range(3):
        term = taps[shift] * ext[pl.ds(ct * pitch + i * 8 + (8 - shift), 8), :]
        if shift and masks is not None:
            term = term * masks[shift - 1]
        terms.append(term)
    return terms[0] + terms[1] + terms[2]


def at_starts(firsts, first_pos, block_len, tile_len, redo):
    for first in firsts:
        for after in range(2):
            place = first + after - first_pos

            @pl.when((place >= 0) & (place < block_len))
            def _():
                redo(place // tile_len)


def tile_masks(firsts, base):
    pos = base + lax.broadcasted_iota(jnp.int32, (8, LANES), 0)
    start = jnp.zeros((8, LANES), jnp.int32)
    for first in firsts:
        start = jnp.maximum(start, jnp.where(first <= pos, first, 0))
    return [pos - shift >= start for shift in (1, 2)]


def load_tiles(raw, stream_ref):
    block_len = stream_ref.shape[1]

    def step(i, _):
        rows = pl.ds(pl.multiple_of(i * 16, 16), 16)
        for ct in range(8):
            tile = stream_ref[0, rows, pl.ds(ct * LANES, LANES)].astype(jnp.float32)
            raw[pl.ds(pl.multiple_of(i * 128 + ct * 8, 8), 8), :] = tile[0:8]
            raw[pl.ds(pl.multiple_of(i * 128 + 64 + ct * 8, 8), 8), :] = tile[8:16]
        return 0

    lax.fori_loop(0, block_len // 16, step, 0, unroll=2)


def bank_taps(filter_ref, turn, stream_id, bank_table, slot):
    for ct in range(8):
        turn[pl.ds(ct * 8, 3), :] = filter_ref[stream_id, :, pl.ds(ct * LANES, LANES)]
    taps = [turn[pl.ds(shift, 8, stride=8), :] for shift in range(3)]
    width = bank_table.shape[0] // 3
    zero = jnp.zeros((8, LANES), jnp.float32)
    for bank, pair in enumerate(((taps[1], taps[2]), (zero, zero), (taps[1], zero))):
        for n in range(2):
            bank_table[pl.ds(bank * width + (slot * 2 + n) * 8, 8), :] = pair[n]
    return taps[0]


def filtered_token(tap, bank_table, bank_row, slot, now, back_1, back_2):
    tap_1 = bank_table[pl.ds(bank_row + slot * 16, 8), :]
    tap_2 = bank_table[pl.ds(bank_row + slot * 16 + 8, 8), :]
    return tap * now + tap_1 * back_1 + tap_2 * back_2


def to_sublanes(ref, scratch, row_count, first_col=0):
    for top in range(0, row_count, 8):
        for ct in range(8):
            scratch[pl.ds(top * 8 + ct * 8, 8), :] = ref[
                top : top + 8, pl.ds(first_col + ct * LANES, LANES)
            ]
    return [scratch[pl.ds((p // 8) * 64 + p % 8, 8, stride=8), :] for p in range(row_count)]


def recur_kernel(
    blocks, groups,
    lengths_ref, tail_ref, k_ref, v_ref, filter_ref, rate_ref, residue_ref, direct_ref,
    y_ref, edge_ref, rate_out, weight_out, in_ref,
    raw_k, raw_v, turn, table, tap_table, ends,
    packed, landed, outbox, inbox, edge_send, edge_recv, send_sem, recv_sem,
):
    block_len = k_ref.shape[1]
    poles = rate_ref.shape[0]
    span = poles * 8
    group = pl.program_id(0)
    me = lax.axis_index("seq")
    first_pos = me * block_len
    firsts = doc_firsts(lengths_ref)
    rounds = max(1, (blocks - 1).bit_length())
    half = packed.shape[1]

    def last_start(pos):
        best = jnp.int32(0)
        for first in firsts:
            best = jnp.maximum(best, jnp.where(first <= pos, first, 0))
        return best

    edge_copy = pltpu.make_async_remote_copy(
        src_ref=packed,
        dst_ref=landed,
        send_sem=edge_send,
        recv_sem=edge_recv,
        device_id={"seq": me + 1},
        device_id_type=MESH,
    )

    def state_copy(k, piece):
        rows = pl.ds(pl.multiple_of(piece * span, span), span)
        return pltpu.make_async_remote_copy(
            src_ref=outbox.at[k, rows],
            dst_ref=inbox.at[k, rows],
            send_sem=send_sem.at[k, piece],
            recv_sem=recv_sem.at[k, piece],
            device_id={"seq": me + (1 << k)},
            device_id_type=MESH,
        )

    own_keep = jnp.where(last_start(first_pos + block_len - 1) < first_pos, 1.0, 0.0)

    def send(k, piece):
        rows = pl.ds(pl.multiple_of(piece * span, span), span)

        @pl.when(me + (1 << k) < blocks)
        def _():
            whole = ends[rows, :]
            if k:
                fade = jnp.exp(-rate_out[rows, :] * float(block_len)) * own_keep
                whole = whole + fade * in_ref[rows, :]
            outbox[k, rows, :] = whole.astype(jnp.bfloat16)
            state_copy(k, piece).start()

    def receive(k, piece):
        rows = pl.ds(pl.multiple_of(piece * span, span), span)
        reach = 1 << k
        far = first_pos - (reach - 1) * block_len

        @pl.when(me >= reach)
        def _():
            state_copy(k, piece).wait_recv()
            got = inbox[k, rows, :].astype(jnp.float32)
            if k:
                clear = jnp.where(last_start(first_pos - 1) < far, 1.0, 0.0)
                got = got * (jnp.exp(-rate_out[rows, :] * float((reach - 1) * block_len)) * clear)
            in_ref[rows, :] += got

    def relay(k, piece):
        receive(k, piece)
        if k + 1 < rounds:
            send(k + 1, piece)

    @pl.when(group == 0)
    def _():
        rows = []
        for side in range(2):
            cols = pl.ds(side * half, half)
            for j in range(3):
                rows.append(tail_ref[j, :, cols].astype(jnp.float32)[14:16])
            rows.append(jnp.zeros((2, half), jnp.float32))
        packed[...] = jnp.concatenate(rows, axis=0).astype(jnp.bfloat16)
        peers = []
        for k in range(rounds):
            peers.append(("seq", me + (1 << k), me + (1 << k) < blocks))
            peers.append(("seq", me - (1 << k), me >= (1 << k)))
        greet(peers)

        @pl.when(me < blocks - 1)
        def _():
            edge_copy.start()

        in_ref[...] = jnp.zeros_like(in_ref)
        table[pl.ds(span, span), :] = jnp.zeros((span, LANES), jnp.float32)

    load_tiles(raw_k, k_ref)
    load_tiles(raw_v, v_ref)

    rates = to_sublanes(rate_ref, turn, poles)
    decays = [jnp.exp(-r) for r in rates]
    own = pl.multiple_of(group * span, span)
    for p in range(poles):
        rate_out[pl.ds(own + p * 8, 8), :] = rates[p]
        table[pl.ds(p * 8, 8), :] = decays[p]
    residues = to_sublanes(residue_ref, turn, poles)
    weights = [residues[p] * (1.0 - decays[p]) for p in range(poles)]
    for p in range(poles):
        weight_out[pl.ds(own + p * 8, 8), :] = weights[p]
    for ct in range(8):
        turn[pl.ds(ct * 8, 8), :] = jnp.broadcast_to(direct_ref[:, pl.ds(ct * LANES, LANES)], (8, LANES))
    direct = turn[pl.ds(0, 8, stride=8), :]

    @pl.when(group == 0)
    def _():
        @pl.when(me > 0)
        def _():
            edge_copy.wait_recv()
            got = landed[...].astype(jnp.float32)
            edge_ref[:, pl.ds(0, half)] = got[0:8]
            edge_ref[:, pl.ds(half, half)] = got[8:16]

        @pl.when(me == 0)
        def _():
            edge_ref[...] = jnp.zeros_like(edge_ref)

    edges = to_sublanes(edge_ref, turn, 8, pl.multiple_of(group * GROUP, GROUP))
    k_tap = bank_taps(filter_ref, turn, 1, tap_table, 0)
    v_tap = bank_taps(filter_ref, turn, 2, tap_table, 1)

    def chunk(i, carry):
        states, (k_1, k_2, v_1, v_2) = list(carry[:poles]), carry[poles:]
        place = first_pos + i * 8
        after = any_between(firsts, place - 1, place)
        for j in range(8):
            rows = pl.ds(i * 64 + j, 8, stride=8)
            starts = any_between(firsts, place + j, place + j + 1)
            bank = jnp.where(starts, span, 0)
            tap_row = jnp.where(starts, 32, jnp.where(after, 64, 0))
            after = starts
            k_0, v_0 = raw_k[rows, :], raw_v[rows, :]
            k = filtered_token(k_tap, tap_table, tap_row, 0, k_0, k_1, k_2)
            v = filtered_token(v_tap, tap_table, tap_row, 1, v_0, v_1, v_2)
            k_1, k_2, v_1, v_2 = k_0, k_1, v_0, v_1
            x = k * v
            sums = [direct * x, None, None, None]
            for p in range(poles):
                states[p] = table[pl.ds(bank + p * 8, 8), :] * states[p] + x
                term = weights[p] * states[p]
                sums[p % 4] = term if sums[p % 4] is None else sums[p % 4] + term
            y_ref[0, rows, :] = (sums[0] + sums[1]) + (sums[2] + sums[3])
        return tuple(states) + (k_1, k_2, v_1, v_2)

    chunks = block_len // 8
    states = tuple(jnp.zeros((8, LANES), jnp.float32) for _ in range(poles))
    states += (edges[3], edges[2], edges[5], edges[4])
    states = lax.fori_loop(0, chunks // 2, chunk, states)
    for k in range(0, rounds, 2):
        piece = group - 1 - k // 2

        @pl.when(piece >= 0)
        def _():
            relay(k, piece)

    states = lax.fori_loop(chunks // 2, chunks, chunk, states)
    for p in range(poles):
        ends[pl.ds(own + p * 8, 8), :] = states[p]
    send(0, group)
    for k in range(1, rounds, 2):
        piece = group - (k + 1) // 2

        @pl.when(piece >= 0)
        def _():
            relay(k, piece)

    @pl.when(group == groups - 1)
    def _():
        for slot in range(2 * groups, 2 * groups + rounds):
            for k in reversed(range(rounds)):
                piece, odd = divmod(slot - 2 - k, 2)
                if odd == 0 and 0 <= piece < groups:
                    relay(k, piece)
        for k in range(rounds):
            for piece in range(groups):

                @pl.when(me + (1 << k) < blocks)
                def _():
                    state_copy(k, piece).wait_send()

        @pl.when(me < blocks - 1)
        def _():
            edge_copy.wait_send()


def finish_kernel(
    lengths_ref, q_ref, edge_ref, filter_ref, rate_ref, weight_ref, in_ref, y_in, unembed_ref,
    gated_ref, logits_ref,
    ext_q, y, total,
):
    block_len = q_ref.shape[1]
    poles = rate_ref.shape[0] // 8
    first_pos = lax.axis_index("seq") * block_len
    firsts = doc_firsts(lengths_ref)
    group = pl.program_id(0)
    cut = jnp.int32(block_len)
    for first in firsts:
        cut = jnp.where(first >= first_pos, jnp.minimum(cut, first - first_pos), cut)
    load_block(ext_q, q_ref)
    load_edge(ext_q, edge_ref, 0)
    tiles = [pl.ds(p * 8, 8) for p in range(poles)]
    decays = [jnp.exp(-rate_ref[tile, :]) for tile in tiles]
    fading = tuple(weight_ref[tile, :] * in_ref[tile, :] * d for tile, d in zip(tiles, decays))

    def fade_chunk(i, fading):
        fading = list(fading)
        for j in range(8):
            sums = [fading[0], fading[1], fading[2], fading[3]]
            for p in range(4, poles):
                sums[p % 4] = sums[p % 4] + fading[p]
            arrived = (sums[0] + sums[1]) + (sums[2] + sums[3])
            rows = pl.ds(i * 64 + j, 8, stride=8)
            y[rows, :] = jnp.where(i * 8 + j < cut, 1.0, 0.0) * arrived
            fading = [f * d for f, d in zip(fading, decays)]
        return tuple(fading)

    carried = (cut + 7) // 8
    lax.fori_loop(0, carried, fade_chunk, fading)

    def plain_chunk(i, _):
        rows = pl.ds(pl.multiple_of(i * 64, 64), 64)
        y[rows, :] = jnp.zeros((64, LANES), jnp.float32)
        return 0

    lax.fori_loop(carried, block_len // 8, plain_chunk, 0)

    def gate(i, ct, taps, masks):
        halves = []
        for side in range(2):
            tile = i * 2 + side
            q = filter_tile(ext_q, taps, tile, ct, masks[side])
            rows = pl.ds(pl.multiple_of(tile * 64 + ct * 8, 8), 8)
            halves.append(q * (y_in[0, rows, :] + y[rows, :]))
        both = jnp.concatenate(halves, axis=0).astype(jnp.bfloat16)
        gated_ref[pl.ds(pl.multiple_of(i * 16, 16), 16), pl.ds(ct * LANES, LANES)] = both

    for ct in range(8):
        taps = load_taps(filter_ref, 0, ct)

        def gate_step(i, _):
            gate(i, ct, taps, [None, None])
            return 0

        lax.fori_loop(0, block_len // 16, gate_step, 0, unroll=4)

    def regate(i):
        masks = []
        for side in range(2):
            pair = tile_masks(firsts, first_pos + i * 16 + side * 8)
            masks.append([jnp.where(m, 1.0, 0.0) for m in pair])
        for ct in range(8):
            gate(i, ct, load_taps(filter_ref, 0, ct), masks)

    at_starts(firsts, first_pos, block_len, 16, regate)
    part = jnp.dot(gated_ref[...], unembed_ref[...], preferred_element_type=jnp.float32)

    @pl.when(group == 0)
    def _():
        total[...] = part

    @pl.when(group > 0)
    def _():
        total[...] += part

    @pl.when(group == pl.num_programs(0) - 1)
    def _():
        logits_ref[...] = total[...].astype(jnp.bfloat16)


def loss_kernel(parts, logits_ref, target_ref, loss_ref, inbox, send_sem, recv_sem):
    me = lax.axis_index("chan")
    others = [lax.rem(me + d, parts) for d in range(1, parts)]
    greet([("chan", other, me >= 0) for other in others])
    copies = []
    for d in range(1, parts):
        copies.append(
            pltpu.make_async_remote_copy(
                src_ref=logits_ref,
                dst_ref=inbox.at[me],
                send_sem=send_sem.at[d - 1],
                recv_sem=recv_sem.at[d - 1],
                device_id={"chan": others[d - 1]},
                device_id_type=MESH,
            )
        )
        copies[-1].start()
    inbox[me] = logits_ref[...]
    for copy in copies:
        copy.wait_recv()
    block_len, vocab = logits_ref.shape
    eye = lax.broadcasted_iota(jnp.int32, (LANES, LANES), 0) == lax.broadcasted_iota(
        jnp.int32, (LANES, LANES), 1
    )
    vocab_ids = lax.broadcasted_iota(jnp.int32, (LANES, vocab), 1)
    for tile in range(block_len // LANES):
        rows = pl.ds(tile * LANES, LANES)
        logits = inbox[0, rows, :].astype(jnp.float32)
        for part in range(1, parts):
            logits = logits + inbox[part, rows, :].astype(jnp.float32)
        wanted = jnp.where(eye, target_ref[tile : tile + 1, :].astype(jnp.float32), 0.0)
        wanted = jnp.sum(wanted, axis=1, keepdims=True).astype(jnp.int32)
        peak = jnp.max(logits, axis=1, keepdims=True)
        exp_total = jnp.sum(jnp.exp(logits - peak), axis=1, keepdims=True)
        picked = jnp.sum(jnp.where(vocab_ids == wanted, logits, 0.0), axis=1, keepdims=True)
        loss = peak + jnp.log(exp_total) - picked
        loss_ref[tile : tile + 1, :] = jnp.sum(jnp.where(eye, loss, 0.0), axis=0, keepdims=True)
    for copy in copies:
        copy.wait_send()


def local(blocks, parts, streams, short_filter, pole_rates, residues, direct, doc_lengths, targets, unembed):
    block_len, chans = streams.shape[1], streams.shape[2]
    poles, vocab = pole_rates.shape[0], unembed.shape[1]
    groups = chans // GROUP
    f32, bf16 = jnp.float32, jnp.bfloat16
    shape = jax.ShapeDtypeStruct
    vmem = pl.BlockSpec(memory_space=pltpu.VMEM)
    smem = pl.BlockSpec(memory_space=pltpu.SMEM)
    params = functools.partial(pltpu.CompilerParams, vmem_limit_bytes=VMEM_LIMIT)

    def stream_spec(j):
        return pl.BlockSpec((1, block_len, GROUP), lambda g: (j, 0, g))

    rounds = max(1, (blocks - 1).bit_length())
    rows = poles * groups * 8
    filter_spec = pl.BlockSpec((3, 3, GROUP), lambda g: (0, 0, g))
    pole_spec = pl.BlockSpec((poles, GROUP), lambda g: (0, g))
    rows_spec = pl.BlockSpec((rows, LANES), lambda g: (0, 0))
    y_spec = pl.BlockSpec((1, block_len * 8, LANES), lambda g: (g, 0, 0))

    y_local, edges, rates, weights, incoming = pl.pallas_call(
        functools.partial(recur_kernel, blocks, groups),
        name="recur",
        grid=(groups,),
        out_shape=[
            shape((groups, block_len * 8, LANES), f32),
            shape((8, chans), f32),
            shape((rows, LANES), f32),
            shape((rows, LANES), f32),
            shape((rows, LANES), f32),
        ],
        in_specs=[
            smem,
            pl.BlockSpec((3, 16, chans), lambda g: (0, block_len // 16 - 1, 0)),
            stream_spec(1), stream_spec(2), filter_spec, pole_spec, pole_spec,
            pl.BlockSpec((1, GROUP), lambda g: (0, g)),
        ],
        out_specs=[y_spec, pl.BlockSpec((8, chans), lambda g: (0, 0)), rows_spec, rows_spec, rows_spec],
        scratch_shapes=[
            pltpu.VMEM((block_len * 8, LANES), f32),
            pltpu.VMEM((block_len * 8, LANES), f32),
            pltpu.VMEM((poles * 8, LANES), f32),
            pltpu.VMEM((2 * poles * 8, LANES), f32),
            pltpu.VMEM((96, LANES), f32),
            pltpu.VMEM((rows, LANES), f32),
            pltpu.VMEM((16, chans // 2), bf16),
            pltpu.VMEM((16, chans // 2), bf16),
            pltpu.VMEM((rounds, rows, LANES), bf16),
            pltpu.VMEM((rounds, rows, LANES), bf16),
            pltpu.SemaphoreType.DMA,
            pltpu.SemaphoreType.DMA,
            pltpu.SemaphoreType.DMA((rounds, groups)),
            pltpu.SemaphoreType.DMA((rounds, groups)),
        ],
        compiler_params=params(collective_id=0, has_side_effects=True),
    )(doc_lengths, streams, streams, streams, short_filter, pole_rates, residues, direct.reshape(1, chans))

    turned_spec = pl.BlockSpec((poles * 8, LANES), lambda g: (g, 0))
    edge_spec = pl.BlockSpec((8, GROUP), lambda g: (0, g))
    gated_out, logits = pl.pallas_call(
        finish_kernel,
        name="finish",
        grid=(groups,),
        out_shape=[shape((block_len, chans), bf16), shape((block_len, vocab), bf16)],
        in_specs=[
            smem, stream_spec(0), edge_spec, filter_spec, turned_spec, turned_spec, turned_spec, y_spec,
            pl.BlockSpec((GROUP, vocab), lambda g: (g, 0)),
        ],
        out_specs=[
            pl.BlockSpec((block_len, GROUP), lambda g: (0, g)),
            pl.BlockSpec((block_len, vocab), lambda g: (0, 0)),
        ],
        scratch_shapes=[
            pltpu.VMEM((8 * (block_len + 8), LANES), f32),
            pltpu.VMEM((block_len * 8, LANES), f32),
            pltpu.VMEM((block_len, vocab), f32),
        ],
        compiler_params=params(),
    )(
        doc_lengths, streams, edges, short_filter, rates, weights,
        incoming, y_local, unembed,
    )

    loss = pl.pallas_call(
        functools.partial(loss_kernel, parts),
        name="loss",
        out_shape=shape((block_len // LANES, LANES), f32),
        in_specs=[vmem, vmem],
        out_specs=vmem,
        scratch_shapes=[
            pltpu.VMEM((parts, block_len, vocab), bf16),
            pltpu.SemaphoreType.DMA((max(1, parts - 1),)),
            pltpu.SemaphoreType.DMA((max(1, parts - 1),)),
        ],
        compiler_params=pltpu.CompilerParams(
            collective_id=1, has_side_effects=True, vmem_limit_bytes=LOSS_VMEM_LIMIT
        ),
    )(logits, targets.reshape(block_len // LANES, LANES))
    return gated_out, loss.reshape(block_len)


def solution(mesh):
    in_specs = (
        P(None, "seq", "chan"),
        P(None, None, "chan"),
        P(None, "chan"),
        P(None, "chan"),
        P("chan"),
        P(),
        P("seq"),
        P("chan", None),
    )
    out_specs = (P("seq", "chan"), P("seq"))
    body = functools.partial(local, mesh.shape["seq"], mesh.shape["chan"])
    return jax.shard_map(body, mesh=mesh, in_specs=in_specs, out_specs=out_specs, check_vma=False)
```

```python
import functools

import jax
import jax.numpy as jnp
from jax import lax
from jax.experimental import pallas as pl
from jax.experimental.pallas import tpu as pltpu
from jax.sharding import PartitionSpec as P

MESH = pl.DeviceIdType.MESH
LANES = 128
GROUP = 8 * LANES
VMEM_LIMIT = 65200 * 1024
LOSS_VMEM_LIMIT = 40 * 1024 * 1024


def doc_firsts(lengths_ref):
    firsts = [jnp.int32(0)]
    for d in range(lengths_ref.shape[0] - 1):
        firsts.append(firsts[-1] + lengths_ref[d])
    return firsts


def any_between(firsts, low, high):
    found = jnp.bool_(False)
    for first in firsts:
        found = found | ((first >= low) & (first < high))
    return found


def greet(peers):
    barrier = pltpu.get_barrier_semaphore()
    for axis, peer, there in peers:

        @pl.when(there)
        def _():
            pl.semaphore_signal(barrier, inc=1, device_id={axis: peer}, device_id_type=MESH)

    if peers:
        pl.semaphore_wait(barrier, sum(jnp.where(there, 1, 0) for _, _, there in peers))


def load_edge(ext, edge_ref, stream_id, first_col=0):
    pitch = ext.shape[0] // 8
    for ct in range(8):
        edge = edge_ref[:, pl.ds(first_col + ct * LANES, LANES)]
        both = jnp.concatenate([edge[0:6], edge[2 * stream_id : 2 * stream_id + 2]], axis=0)
        ext[pl.ds(ct * pitch, 8), :] = both


def load_block(ext, stream_ref):
    block_len = stream_ref.shape[1]
    pitch = block_len + 8

    def step(i, _):
        rows = pl.ds(pl.multiple_of(i * 16, 16), 16)
        for ct in range(8):
            tile = stream_ref[0, rows, pl.ds(ct * LANES, LANES)].astype(jnp.float32)
            ext[pl.ds(pl.multiple_of(ct * pitch + i * 16 + 8, 8), 16), :] = tile
        return 0

    lax.fori_loop(0, block_len // 16, step, 0)


def load_taps(filter_ref, stream_id, ct):
    cols = pl.ds(ct * LANES, LANES)
    return [
        jnp.broadcast_to(filter_ref[stream_id, shift : shift + 1, cols], (8, LANES)) for shift in range(3)
    ]


def filter_tile(ext, taps, i, ct, masks=None):
    pitch = ext.shape[0] // 8
    terms = []
    for shift in range(3):
        term = taps[shift] * ext[pl.ds(ct * pitch + i * 8 + (8 - shift), 8), :]
        if shift and masks is not None:
            term = term * masks[shift - 1]
        terms.append(term)
    return terms[0] + terms[1] + terms[2]


def at_starts(firsts, first_pos, block_len, tile_len, redo):
    for first in firsts:
        for after in range(2):
            place = first + after - first_pos

            @pl.when((place >= 0) & (place < block_len))
            def _():
                redo(place // tile_len)


def tile_masks(firsts, base):
    pos = base + lax.broadcasted_iota(jnp.int32, (8, LANES), 0)
    start = jnp.zeros((8, LANES), jnp.int32)
    for first in firsts:
        start = jnp.maximum(start, jnp.where(first <= pos, first, 0))
    return [pos - shift >= start for shift in (1, 2)]


def load_tiles(raw, stream_ref):
    block_len = stream_ref.shape[1]

    def step(i, _):
        rows = pl.ds(pl.multiple_of(i * 16, 16), 16)
        for ct in range(8):
            tile = stream_ref[0, rows, pl.ds(ct * LANES, LANES)].astype(jnp.float32)
            raw[pl.ds(pl.multiple_of(i * 128 + ct * 8, 8), 8), :] = tile[0:8]
            raw[pl.ds(pl.multiple_of(i * 128 + 64 + ct * 8, 8), 8), :] = tile[8:16]
        return 0

    lax.fori_loop(0, block_len // 16, step, 0, unroll=2)


def bank_taps(filter_ref, turn, stream_id, bank_table, slot):
    for ct in range(8):
        turn[pl.ds(ct * 8, 3), :] = filter_ref[stream_id, :, pl.ds(ct * LANES, LANES)]
    taps = [turn[pl.ds(shift, 8, stride=8), :] for shift in range(3)]
    width = bank_table.shape[0] // 3
    zero = jnp.zeros((8, LANES), jnp.float32)
    for bank, pair in enumerate(((taps[1], taps[2]), (zero, zero), (taps[1], zero))):
        for n in range(2):
            bank_table[pl.ds(bank * width + (slot * 2 + n) * 8, 8), :] = pair[n]
    return taps[0]


def filtered_token(tap, bank_table, bank_row, slot, now, back_1, back_2):
    tap_1 = bank_table[pl.ds(bank_row + slot * 16, 8), :]
    tap_2 = bank_table[pl.ds(bank_row + slot * 16 + 8, 8), :]
    return tap * now + tap_1 * back_1 + tap_2 * back_2


def to_sublanes(ref, scratch, row_count, first_col=0):
    for top in range(0, row_count, 8):
        for ct in range(8):
            scratch[pl.ds(top * 8 + ct * 8, 8), :] = ref[
                top : top + 8, pl.ds(first_col + ct * LANES, LANES)
            ]
    return [scratch[pl.ds((p // 8) * 64 + p % 8, 8, stride=8), :] for p in range(row_count)]


def recur_kernel(
    blocks, groups,
    lengths_ref, tail_ref, k_ref, v_ref, filter_ref, rate_ref, residue_ref, direct_ref,
    y_ref, edge_ref, rate_out, weight_out, in_ref,
    raw_k, raw_v, turn, table, tap_table, ends,
    packed, landed, outbox, inbox, edge_send, edge_recv, send_sem, recv_sem,
):
    block_len = k_ref.shape[1]
    poles = rate_ref.shape[0]
    span = poles * 8
    group = pl.program_id(0)
    me = lax.axis_index("seq")
    first_pos = me * block_len
    firsts = doc_firsts(lengths_ref)
    rounds = max(1, (blocks - 1).bit_length())
    half = packed.shape[1]

    def last_start(pos):
        best = jnp.int32(0)
        for first in firsts:
            best = jnp.maximum(best, jnp.where(first <= pos, first, 0))
        return best

    edge_copy = pltpu.make_async_remote_copy(
        src_ref=packed,
        dst_ref=landed,
        send_sem=edge_send,
        recv_sem=edge_recv,
        device_id={"seq": me + 1},
        device_id_type=MESH,
    )

    def state_copy(k, piece):
        rows = pl.ds(pl.multiple_of(piece * span, span), span)
        return pltpu.make_async_remote_copy(
            src_ref=outbox.at[k, rows],
            dst_ref=inbox.at[k, rows],
            send_sem=send_sem.at[k, piece],
            recv_sem=recv_sem.at[k, piece],
            device_id={"seq": me + (1 << k)},
            device_id_type=MESH,
        )

    own_keep = jnp.where(last_start(first_pos + block_len - 1) < first_pos, 1.0, 0.0)

    def send(k, piece):
        rows = pl.ds(pl.multiple_of(piece * span, span), span)

        @pl.when(me + (1 << k) < blocks)
        def _():
            whole = ends[rows, :]
            if k:
                fade = jnp.exp(-rate_out[rows, :] * float(block_len)) * own_keep
                whole = whole + fade * in_ref[rows, :]
            outbox[k, rows, :] = whole.astype(jnp.bfloat16)
            state_copy(k, piece).start()

    def receive(k, piece):
        rows = pl.ds(pl.multiple_of(piece * span, span), span)
        reach = 1 << k
        far = first_pos - (reach - 1) * block_len

        @pl.when(me >= reach)
        def _():
            state_copy(k, piece).wait_recv()
            got = inbox[k, rows, :].astype(jnp.float32)
            if k:
                clear = jnp.where(last_start(first_pos - 1) < far, 1.0, 0.0)
                got = got * (jnp.exp(-rate_out[rows, :] * float((reach - 1) * block_len)) * clear)
            in_ref[rows, :] += got

    def relay(k, piece):
        receive(k, piece)
        if k + 1 < rounds:
            send(k + 1, piece)

    @pl.when(group == 0)
    def _():
        rows = []
        for side in range(2):
            cols = pl.ds(side * half, half)
            for j in range(3):
                rows.append(tail_ref[j, :, cols].astype(jnp.float32)[14:16])
            rows.append(jnp.zeros((2, half), jnp.float32))
        packed[...] = jnp.concatenate(rows, axis=0).astype(jnp.bfloat16)
        peers = []
        for k in range(rounds):
            peers.append(("seq", me + (1 << k), me + (1 << k) < blocks))
            peers.append(("seq", me - (1 << k), me >= (1 << k)))
        greet(peers)

        @pl.when(me < blocks - 1)
        def _():
            edge_copy.start()

        in_ref[...] = jnp.zeros_like(in_ref)
        table[pl.ds(span, span), :] = jnp.zeros((span, LANES), jnp.float32)

    load_tiles(raw_k, k_ref)
    load_tiles(raw_v, v_ref)

    rates = to_sublanes(rate_ref, turn, poles)
    decays = [jnp.exp(-r) for r in rates]
    own = pl.multiple_of(group * span, span)
    for p in range(poles):
        rate_out[pl.ds(own + p * 8, 8), :] = rates[p]
        table[pl.ds(p * 8, 8), :] = decays[p]
    residues = to_sublanes(residue_ref, turn, poles)
    weights = [residues[p] * (1.0 - decays[p]) for p in range(poles)]
    for p in range(poles):
        weight_out[pl.ds(own + p * 8, 8), :] = weights[p]
    for ct in range(8):
        turn[pl.ds(ct * 8, 8), :] = jnp.broadcast_to(direct_ref[:, pl.ds(ct * LANES, LANES)], (8, LANES))
    direct = turn[pl.ds(0, 8, stride=8), :]

    @pl.when(group == 0)
    def _():
        @pl.when(me > 0)
        def _():
            edge_copy.wait_recv()
            got = landed[...].astype(jnp.float32)
            edge_ref[:, pl.ds(0, half)] = got[0:8]
            edge_ref[:, pl.ds(half, half)] = got[8:16]

        @pl.when(me == 0)
        def _():
            edge_ref[...] = jnp.zeros_like(edge_ref)

    edges = to_sublanes(edge_ref, turn, 8, pl.multiple_of(group * GROUP, GROUP))
    k_tap = bank_taps(filter_ref, turn, 1, tap_table, 0)
    v_tap = bank_taps(filter_ref, turn, 2, tap_table, 1)

    def chunk(i, carry):
        states, (k_1, k_2, v_1, v_2) = list(carry[:poles]), carry[poles:]
        place = first_pos + i * 8
        after = any_between(firsts, place - 1, place)
        for j in range(8):
            rows = pl.ds(i * 64 + j, 8, stride=8)
            starts = any_between(firsts, place + j, place + j + 1)
            bank = jnp.where(starts, span, 0)
            tap_row = jnp.where(starts, 32, jnp.where(after, 64, 0))
            after = starts
            k_0, v_0 = raw_k[rows, :], raw_v[rows, :]
            k = filtered_token(k_tap, tap_table, tap_row, 0, k_0, k_1, k_2)
            v = filtered_token(v_tap, tap_table, tap_row, 1, v_0, v_1, v_2)
            k_1, k_2, v_1, v_2 = k_0, k_1, v_0, v_1
            x = k * v
            sums = [direct * x, None, None, None]
            for p in range(poles):
                states[p] = table[pl.ds(bank + p * 8, 8), :] * states[p] + x
                term = weights[p] * states[p]
                sums[p % 4] = term if sums[p % 4] is None else sums[p % 4] + term
            y_ref[0, rows, :] = (sums[0] + sums[1]) + (sums[2] + sums[3])
        return tuple(states) + (k_1, k_2, v_1, v_2)

    chunks = block_len // 8
    states = tuple(jnp.zeros((8, LANES), jnp.float32) for _ in range(poles))
    states += (edges[3], edges[2], edges[5], edges[4])
    states = lax.fori_loop(0, chunks // 2, chunk, states, unroll=2)
    for k in range(0, rounds, 2):
        piece = group - 1 - k // 2

        @pl.when(piece >= 0)
        def _():
            relay(k, piece)

    states = lax.fori_loop(chunks // 2, chunks, chunk, states, unroll=2)
    for p in range(poles):
        ends[pl.ds(own + p * 8, 8), :] = states[p]
    send(0, group)
    for k in range(1, rounds, 2):
        piece = group - (k + 1) // 2

        @pl.when(piece >= 0)
        def _():
            relay(k, piece)

    @pl.when(group == groups - 1)
    def _():
        for slot in range(2 * groups, 2 * groups + rounds):
            for k in reversed(range(rounds)):
                piece, odd = divmod(slot - 2 - k, 2)
                if odd == 0 and 0 <= piece < groups:
                    relay(k, piece)
        for k in range(rounds):
            for piece in range(groups):

                @pl.when(me + (1 << k) < blocks)
                def _():
                    state_copy(k, piece).wait_send()

        @pl.when(me < blocks - 1)
        def _():
            edge_copy.wait_send()


def finish_kernel(
    lengths_ref, q_ref, edge_ref, filter_ref, rate_ref, weight_ref, in_ref, y_in, unembed_ref,
    gated_ref, logits_ref,
    ext_q, y, total,
):
    block_len = q_ref.shape[1]
    poles = rate_ref.shape[0] // 8
    first_pos = lax.axis_index("seq") * block_len
    firsts = doc_firsts(lengths_ref)
    group = pl.program_id(0)
    cut = jnp.int32(block_len)
    for first in firsts:
        cut = jnp.where(first >= first_pos, jnp.minimum(cut, first - first_pos), cut)
    load_block(ext_q, q_ref)
    load_edge(ext_q, edge_ref, 0)
    tiles = [pl.ds(p * 8, 8) for p in range(poles)]
    decays = [jnp.exp(-rate_ref[tile, :]) for tile in tiles]
    fading = tuple(weight_ref[tile, :] * in_ref[tile, :] * d for tile, d in zip(tiles, decays))

    def fade_chunk(i, fading):
        fading = list(fading)
        for j in range(16):
            sums = [fading[0], fading[1], fading[2], fading[3]]
            for p in range(4, poles):
                sums[p % 4] = sums[p % 4] + fading[p]
            arrived = (sums[0] + sums[1]) + (sums[2] + sums[3])
            rows = pl.ds(i * 128 + j // 8 * 64 + j % 8, 8, stride=8)
            y[rows, :] = jnp.where(i * 16 + j < cut, 1.0, 0.0) * arrived
            fading = [f * d for f, d in zip(fading, decays)]
        return tuple(fading)

    carried = (cut + 15) // 16
    lax.fori_loop(0, carried, fade_chunk, fading)

    def plain_chunk(i, _):
        rows = pl.ds(pl.multiple_of(i * 128, 128), 128)
        y[rows, :] = jnp.zeros((128, LANES), jnp.float32)
        return 0

    lax.fori_loop(carried, block_len // 16, plain_chunk, 0)

    def gate(i, ct, taps, masks):
        halves = []
        for side in range(2):
            tile = i * 2 + side
            q = filter_tile(ext_q, taps, tile, ct, masks[side])
            rows = pl.ds(pl.multiple_of(tile * 64 + ct * 8, 8), 8)
            halves.append(q * (y_in[0, rows, :] + y[rows, :]))
        both = jnp.concatenate(halves, axis=0).astype(jnp.bfloat16)
        gated_ref[pl.ds(pl.multiple_of(i * 16, 16), 16), pl.ds(ct * LANES, LANES)] = both

    for ct in range(8):
        taps = load_taps(filter_ref, 0, ct)

        def gate_step(i, _):
            gate(i, ct, taps, [None, None])
            return 0

        lax.fori_loop(0, block_len // 16, gate_step, 0, unroll=4)

    def regate(i):
        masks = []
        for side in range(2):
            pair = tile_masks(firsts, first_pos + i * 16 + side * 8)
            masks.append([jnp.where(m, 1.0, 0.0) for m in pair])
        for ct in range(8):
            gate(i, ct, load_taps(filter_ref, 0, ct), masks)

    at_starts(firsts, first_pos, block_len, 16, regate)
    part = jnp.dot(gated_ref[...], unembed_ref[...], preferred_element_type=jnp.float32)

    @pl.when(group == 0)
    def _():
        total[...] = part

    @pl.when(group > 0)
    def _():
        total[...] += part

    @pl.when(group == pl.num_programs(0) - 1)
    def _():
        logits_ref[...] = total[...].astype(jnp.bfloat16)


def loss_kernel(parts, logits_ref, target_ref, loss_ref, inbox, send_sem, recv_sem):
    me = lax.axis_index("chan")
    others = [lax.rem(me + d, parts) for d in range(1, parts)]
    greet([("chan", other, me >= 0) for other in others])
    copies = []
    for d in range(1, parts):
        copies.append(
            pltpu.make_async_remote_copy(
                src_ref=logits_ref,
                dst_ref=inbox.at[me],
                send_sem=send_sem.at[d - 1],
                recv_sem=recv_sem.at[d - 1],
                device_id={"chan": others[d - 1]},
                device_id_type=MESH,
            )
        )
        copies[-1].start()
    inbox[me] = logits_ref[...]
    for copy in copies:
        copy.wait_recv()
    block_len, vocab = logits_ref.shape
    eye = lax.broadcasted_iota(jnp.int32, (LANES, LANES), 0) == lax.broadcasted_iota(
        jnp.int32, (LANES, LANES), 1
    )
    vocab_ids = lax.broadcasted_iota(jnp.int32, (LANES, vocab), 1)
    for tile in range(block_len // LANES):
        rows = pl.ds(tile * LANES, LANES)
        logits = inbox[0, rows, :].astype(jnp.float32)
        for part in range(1, parts):
            logits = logits + inbox[part, rows, :].astype(jnp.float32)
        wanted = jnp.where(eye, target_ref[tile : tile + 1, :].astype(jnp.float32), 0.0)
        wanted = jnp.sum(wanted, axis=1, keepdims=True).astype(jnp.int32)
        peak = jnp.max(logits, axis=1, keepdims=True)
        exp_total = jnp.sum(jnp.exp(logits - peak), axis=1, keepdims=True)
        picked = jnp.sum(jnp.where(vocab_ids == wanted, logits, 0.0), axis=1, keepdims=True)
        loss = peak + jnp.log(exp_total) - picked
        loss_ref[tile : tile + 1, :] = jnp.sum(jnp.where(eye, loss, 0.0), axis=0, keepdims=True)
    for copy in copies:
        copy.wait_send()


def local(blocks, parts, streams, short_filter, pole_rates, residues, direct, doc_lengths, targets, unembed):
    block_len, chans = streams.shape[1], streams.shape[2]
    poles, vocab = pole_rates.shape[0], unembed.shape[1]
    groups = chans // GROUP
    f32, bf16 = jnp.float32, jnp.bfloat16
    shape = jax.ShapeDtypeStruct
    vmem = pl.BlockSpec(memory_space=pltpu.VMEM)
    smem = pl.BlockSpec(memory_space=pltpu.SMEM)
    params = functools.partial(pltpu.CompilerParams, vmem_limit_bytes=VMEM_LIMIT)

    def stream_spec(j):
        return pl.BlockSpec((1, block_len, GROUP), lambda g: (j, 0, g))

    rounds = max(1, (blocks - 1).bit_length())
    rows = poles * groups * 8
    filter_spec = pl.BlockSpec((3, 3, GROUP), lambda g: (0, 0, g))
    pole_spec = pl.BlockSpec((poles, GROUP), lambda g: (0, g))
    rows_spec = pl.BlockSpec((rows, LANES), lambda g: (0, 0))
    y_spec = pl.BlockSpec((1, block_len * 8, LANES), lambda g: (g, 0, 0))

    y_local, edges, rates, weights, incoming = pl.pallas_call(
        functools.partial(recur_kernel, blocks, groups),
        name="recur",
        grid=(groups,),
        out_shape=[
            shape((groups, block_len * 8, LANES), f32),
            shape((8, chans), f32),
            shape((rows, LANES), f32),
            shape((rows, LANES), f32),
            shape((rows, LANES), f32),
        ],
        in_specs=[
            smem,
            pl.BlockSpec((3, 16, chans), lambda g: (0, block_len // 16 - 1, 0)),
            stream_spec(1), stream_spec(2), filter_spec, pole_spec, pole_spec,
            pl.BlockSpec((1, GROUP), lambda g: (0, g)),
        ],
        out_specs=[y_spec, pl.BlockSpec((8, chans), lambda g: (0, 0)), rows_spec, rows_spec, rows_spec],
        scratch_shapes=[
            pltpu.VMEM((block_len * 8, LANES), f32),
            pltpu.VMEM((block_len * 8, LANES), f32),
            pltpu.VMEM((poles * 8, LANES), f32),
            pltpu.VMEM((2 * poles * 8, LANES), f32),
            pltpu.VMEM((96, LANES), f32),
            pltpu.VMEM((rows, LANES), f32),
            pltpu.VMEM((16, chans // 2), bf16),
            pltpu.VMEM((16, chans // 2), bf16),
            pltpu.VMEM((rounds, rows, LANES), bf16),
            pltpu.VMEM((rounds, rows, LANES), bf16),
            pltpu.SemaphoreType.DMA,
            pltpu.SemaphoreType.DMA,
            pltpu.SemaphoreType.DMA((rounds, groups)),
            pltpu.SemaphoreType.DMA((rounds, groups)),
        ],
        compiler_params=params(collective_id=0, has_side_effects=True),
    )(doc_lengths, streams, streams, streams, short_filter, pole_rates, residues, direct.reshape(1, chans))

    turned_spec = pl.BlockSpec((poles * 8, LANES), lambda g: (g, 0))
    edge_spec = pl.BlockSpec((8, GROUP), lambda g: (0, g))
    gated_out, logits = pl.pallas_call(
        finish_kernel,
        name="finish",
        grid=(groups,),
        out_shape=[shape((block_len, chans), bf16), shape((block_len, vocab), bf16)],
        in_specs=[
            smem, stream_spec(0), edge_spec, filter_spec, turned_spec, turned_spec, turned_spec, y_spec,
            pl.BlockSpec((GROUP, vocab), lambda g: (g, 0)),
        ],
        out_specs=[
            pl.BlockSpec((block_len, GROUP), lambda g: (0, g)),
            pl.BlockSpec((block_len, vocab), lambda g: (0, 0)),
        ],
        scratch_shapes=[
            pltpu.VMEM((8 * (block_len + 8), LANES), f32),
            pltpu.VMEM((block_len * 8, LANES), f32),
            pltpu.VMEM((block_len, vocab), f32),
        ],
        compiler_params=params(),
    )(
        doc_lengths, streams, edges, short_filter, rates, weights,
        incoming, y_local, unembed,
    )

    loss = pl.pallas_call(
        functools.partial(loss_kernel, parts),
        name="loss",
        out_shape=shape((block_len // LANES, LANES), f32),
        in_specs=[vmem, vmem],
        out_specs=vmem,
        scratch_shapes=[
            pltpu.VMEM((parts, block_len, vocab), bf16),
            pltpu.SemaphoreType.DMA((max(1, parts - 1),)),
            pltpu.SemaphoreType.DMA((max(1, parts - 1),)),
        ],
        compiler_params=pltpu.CompilerParams(
            collective_id=1, has_side_effects=True, vmem_limit_bytes=LOSS_VMEM_LIMIT
        ),
    )(logits, targets.reshape(block_len // LANES, LANES))
    return gated_out, loss.reshape(block_len)


def solution(mesh):
    in_specs = (
        P(None, "seq", "chan"),
        P(None, None, "chan"),
        P(None, "chan"),
        P(None, "chan"),
        P("chan"),
        P(),
        P("seq"),
        P("chan", None),
    )
    out_specs = (P("seq", "chan"), P("seq"))
    body = functools.partial(local, mesh.shape["seq"], mesh.shape["chan"])
    return jax.shard_map(body, mesh=mesh, in_specs=in_specs, out_specs=out_specs, check_vma=False)
```
